512 devices in a mesh: dp: 32 (over z, core), seq: 16 (over x, y).
Axes of the slice: x: 4, y: 4, z: 16, core: 2. Of those that a mesh axis runs over, the one named last changes fastest.
Arguments:
- queries: bfloat16 [1024, 64, 1024], P('seq', 'dp'), may hold values from -8 to 8
- key_rows: bfloat16 [1024, 64, 1024], P('seq', 'dp'), may hold values from -8 to 8
- value_rows: bfloat16 [1024, 64, 1024], P('seq', 'dp'), may hold values from -6 to 6
- cotangent: bfloat16 [1024, 64, 1024], P('seq', 'dp'), may hold values from -6 to 6
- out_weight: bfloat16 [1024, 1024], P('seq'), may hold values from -0.1875 to 0.1875
- node_counts: int32 [64], P('dp'), may hold values from 256 to 1024, as said below
- edge_bits: int32 [64, 8, 1], P('dp'), may hold values from 0 to 255, as said below
Outputs:
- layer_out: bfloat16 [1024, 64, 1024], P('seq', 'dp')
- query_grad: bfloat16 [1024, 64, 1024], P('seq', 'dp')
- key_grad: bfloat16 [1024, 64, 1024], P('seq', 'dp')
- value_grad: bfloat16 [1024, 64, 1024], P('seq', 'dp')
- weight_grad: float32 [1024, 1024], P('seq')
The draws below stay inside these ranges and needn't reach their ends.
Inputs may be any that keep to these rules, and one draw needn't show every extreme that they name: `node_counts`: every count is at least 256; some graph has exactly 1024. `edge_bits`: bits for blocks at or past 8 are 0; every query block sees its own key block and key block 0; in some graph the last query block sees every key block.
All inputs are finite; a program needn't handle non-finite values.
Results may differ from the reference program's by a relative error of at most 0.012.
The reference program's roundings to bfloat16 on the way count: a program that leaves them out, or rounds other values in their place, can miss the bound.
Values may be sent and summed in bfloat16 or wider, within the bound.
A program may use at most 64 MiB of HBM per device.

```python
import math
import jax
import jax.numpy as jnp
from jax import lax

HEAD_DIM = 128
D = 1024
BLOCK = 128
WORD_BITS = 16
NODES = 1024
NB = 8
WORDS = 1
GRAPHS = 64


def draw_queries(key, part):
    key = jax.random.fold_in(key, 11)
    base = jnp.clip(1.5 * jax.random.normal(key, (NODES, GRAPHS, D), jnp.float32), -8.0, 8.0)
    return base.astype(jnp.bfloat16)


def draw_key_rows(key, part):
    key = jax.random.fold_in(key, 12)
    base = jnp.clip(1.5 * jax.random.normal(key, (NODES, GRAPHS, D), jnp.float32), -8.0, 8.0)
    return base.astype(jnp.bfloat16)


def draw_node_counts(key, part):
    key = jax.random.fold_in(key, 21)
    counts = jax.random.randint(key, (GRAPHS,), NODES // 4, NODES + 1, dtype=jnp.int32)
    chosen = jax.random.randint(jax.random.fold_in(key, 1), (), 0, GRAPHS, dtype=jnp.int32)
    return jnp.where(jnp.arange(GRAPHS, dtype=jnp.int32) == chosen, NODES, counts).astype(jnp.int32)


def draw_edge_bits(key, part):
    key = jax.random.fold_in(key, 31)
    drawn = jax.random.randint(key, (GRAPHS, NB, WORDS), 0, 2 ** WORD_BITS, dtype=jnp.int32)
    chosen = jax.random.randint(jax.random.fold_in(key, 1), (), 0, GRAPHS, dtype=jnp.int32)
    row_block = jnp.arange(NB, dtype=jnp.int32)[None, :, None]
    word_index = jnp.arange(WORDS, dtype=jnp.int32)[None, None, :]
    graph_index = jnp.arange(GRAPHS, dtype=jnp.int32)[:, None, None]
    live_bits = jnp.clip(NB - WORD_BITS * word_index, 0, WORD_BITS)
    limit = jnp.left_shift(jnp.int32(1), live_bits) - 1
    own_block = jnp.where(row_block // WORD_BITS == word_index, jnp.left_shift(jnp.int32(1), row_block % WORD_BITS), 0)
    first_block = jnp.where(word_index == 0, 1, 0)
    masked = drawn & limit | own_block | first_block
    full_row = (graph_index == chosen) & (row_block == NB - 1)
    return jnp.where(full_row, limit, masked).astype(jnp.int32)


def level_of(own_key, dims, shards, low, largest):
    gain, own = 1.0, jax.random.fold_in(own_key, 6)
    for position, shards_of in shards:
        heights = jnp.exp(jax.random.uniform(jax.random.fold_in(own, position), (shards_of,), jnp.float32, low / len(shards), largest / len(shards)))
        gain = gain * jnp.repeat(heights, dims[position] // shards_of).reshape([-1 if axis == position else 1 for axis in range(len(dims))])
    return gain


def normal_values(rng, shape, scale, most, pieces=(), held_as=jnp.bfloat16):
    level = level_of(rng, shape, pieces, -0.22, 0.18) if pieces else 1.0
    values = jax.random.normal(rng, shape, jnp.float32) * scale * level
    return jnp.minimum(jnp.maximum(values, -most), most).astype(held_as)


def setup_inputs(seed: int = 0) -> dict:
    streams_of = jax.random.split(jax.random.key(seed), 8)
    return {
        "queries": draw_queries(jax.random.fold_in(streams_of[7], 71), 0),
        "key_rows": draw_key_rows(jax.random.fold_in(streams_of[7], 71), 0),
        "value_rows": normal_values(streams_of[2], (NODES, GRAPHS, D), 1.0, 6.0, ((0, 16), (1, 32))),
        "cotangent": normal_values(streams_of[3], (NODES, GRAPHS, D), 1.0, 6.0, ((0, 16), (1, 32))),
        "out_weight": normal_values(streams_of[4], (D, D), D ** -0.5, 0.1875, ((0, 16),)),
        "node_counts": draw_node_counts(jax.random.fold_in(streams_of[7], 71), 0),
        "edge_bits": draw_edge_bits(jax.random.fold_in(streams_of[7], 71), 0),
    }


def permitted(row_words, col_pos, amount):
    col_block = col_pos // BLOCK
    chosen = jnp.zeros((row_words.shape[0], col_pos.shape[0]), jnp.int32)
    for word_index in range(row_words.shape[1]):
        chosen = jnp.where((col_block // WORD_BITS == word_index)[None, :], row_words[:, word_index:word_index + 1], chosen)
    flag_bits = jnp.right_shift(chosen, (col_block % WORD_BITS)[None, :]) & 1
    return (flag_bits == 1) & (col_pos < amount)[None, :]

def probabilities(query_part, key_all, row_words, amount, score_scale):
    col_pos = jnp.arange(key_all.shape[0], dtype=jnp.int32)
    scores = lax.dot_general(query_part, key_all, (((1,), (1,)), ((), ())), preferred_element_type=jnp.float32) * score_scale
    scores = jnp.where(permitted(row_words, col_pos, amount), scores, -jnp.inf)
    row_top = lax.optimization_barrier(jnp.max(scores, axis=1, keepdims=True))
    weights = jnp.exp(scores - row_top)
    return weights / lax.optimization_barrier(jnp.sum(weights, axis=1, keepdims=True))

def forward_rows(query_part, row_start, key_all, value_all, row_words, amount, score_scale):
    probability = probabilities(query_part, key_all, row_words, amount, score_scale)
    row_pos = row_start + jnp.arange(query_part.shape[0], dtype=jnp.int32)
    mixed = jnp.dot(probability.astype(jnp.bfloat16), value_all, preferred_element_type=jnp.float32)
    return jnp.where((row_pos < amount)[:, None], mixed, 0.0).astype(jnp.bfloat16)

def backward_rows(query_part, att_part, grad_part, key_all, value_all, row_words, amount, score_scale):
    probability = probabilities(query_part, key_all, row_words, amount, score_scale)
    value_share = lax.dot_general(probability.astype(jnp.bfloat16), grad_part, (((0,), (0,)), ((), ())), preferred_element_type=jnp.float32)
    prob_grad = lax.dot_general(grad_part, value_all, (((1,), (1,)), ((), ())), preferred_element_type=jnp.float32)
    centre = lax.optimization_barrier(jnp.sum(grad_part.astype(jnp.float32) * att_part.astype(jnp.float32), axis=1, keepdims=True))
    score_grad = (probability * (prob_grad - centre) * score_scale).astype(jnp.bfloat16)
    query_share = jnp.dot(score_grad, key_all, preferred_element_type=jnp.float32)
    key_share = lax.dot_general(score_grad, query_part, (((0,), (0,)), ((), ())), preferred_element_type=jnp.float32)
    return (query_share, key_share, value_share)

def reference(queries, key_rows, value_rows, cotangent, out_weight, node_counts, edge_bits):
    node_total, graph_total, feature_width = queries.shape
    head_size = HEAD_DIM
    head_count = feature_width // head_size
    score_scale = 1.0 / math.sqrt(head_size)
    block_rows = min(512, node_total)
    block_total = node_total // block_rows

    def to_items(values_in):
        return jnp.transpose(values_in.reshape(node_total, graph_total * head_count, head_size), (1, 0, 2))

    def from_items(values_in):
        return jnp.transpose(values_in, (1, 0, 2)).reshape(node_total, graph_total, feature_width)
    item_counts = jnp.repeat(node_counts, head_count)
    item_bits = jnp.repeat(edge_bits, head_count, axis=0)

    def forward_item(operands):
        query_all, key_all, value_all, amount, block_bits = operands
        row_words = jnp.repeat(block_bits, BLOCK, axis=0)
        return forward_rows(query_all, jnp.int32(0), key_all, value_all, row_words, amount, score_scale)
    query_items = to_items(queries)
    key_items = to_items(key_rows)
    value_items = to_items(value_rows)
    attended_items = lax.map(forward_item, (query_items, key_items, value_items, item_counts, item_bits))
    attended = from_items(attended_items).reshape(node_total * graph_total, feature_width)
    flat_cot = cotangent.reshape(node_total * graph_total, feature_width)
    layer_out = jnp.dot(attended, out_weight, preferred_element_type=jnp.float32).astype(jnp.bfloat16)
    layer_out = layer_out.reshape(node_total, graph_total, feature_width)
    valid_rows = (jnp.arange(node_total, dtype=jnp.int32)[:, None] < node_counts[None, :]).reshape(-1, 1)
    back_sum = lax.dot_general(flat_cot, out_weight, (((1,), (1,)), ((), ())), preferred_element_type=jnp.float32)
    att_grad = jnp.where(valid_rows, back_sum, 0.0).astype(jnp.bfloat16)
    weight_grad = lax.dot_general(attended, flat_cot, (((0,), (0,)), ((), ())), preferred_element_type=jnp.float32)
    weight_grad = weight_grad * (1.0 / math.sqrt(graph_total * node_total))
    grad_items = to_items(att_grad.reshape(node_total, graph_total, feature_width))

    def backward_item(operands):
        query_all, key_all, value_all, att_all, grad_all, amount, block_bits = operands
        row_words = jnp.repeat(block_bits, BLOCK, axis=0)

        def one_block(carried, block_index):
            key_sum, value_sum = carried
            row_start = (block_index * block_rows).astype(jnp.int32)

            def rows_of(values_in):
                return lax.dynamic_slice_in_dim(values_in, row_start, block_rows)
            query_share, key_share, value_share = backward_rows(rows_of(query_all), rows_of(att_all), rows_of(grad_all), key_all, value_all, rows_of(row_words), amount, score_scale)
            return ((key_sum + key_share, value_sum + value_share), query_share.astype(jnp.bfloat16))
        zeros_init = jnp.zeros((node_total, head_size), jnp.float32)
        (key_sum, value_sum), query_blocks = lax.scan(one_block, (zeros_init, zeros_init), jnp.arange(block_total, dtype=jnp.int32))
        return (query_blocks.reshape(node_total, head_size), key_sum.astype(jnp.bfloat16), value_sum.astype(jnp.bfloat16))
    query_grad, key_grad, value_grad = lax.map(backward_item, (query_items, key_items, value_items, attended_items, grad_items, item_counts, item_bits))
    return (layer_out, from_items(query_grad), from_items(key_grad), from_items(value_grad), weight_grad)
```

```python
import functools
import math

import jax
import jax.numpy as jnp
from jax import lax
from jax.experimental import pallas as pl
from jax.experimental.pallas import tpu as pltpu
from jax.sharding import PartitionSpec as P

HEAD = 128
BLOCK = 128
NODES = 1024
WIDTH = 1024
ROWS = 64
IB = 256
MESH = pl.DeviceIdType.MESH
BF = jnp.bfloat16
F32 = jnp.float32
NT = (((1,), (1,)), ((), ()))
MASKED = -1e30


def kernel(
    planes,
    q_ref,
    k_ref,
    v_ref,
    cot_ref,
    w_ref,
    count_ref,
    bits_ref,
    out_ref,
    dq_ref,
    dk_ref,
    dv_ref,
    wg_ref,
    qkv_s,
    cot_s,
    qkv_r,
    aux,
    cot_all,
    w_all,
    scores,
    prob,
    prob_b,
    sgrad,
    att_t,
    att_n,
    ag_n,
    ag_t,
    vt,
    kt,
    dqkv_n,
    att_ret,
    dqkv_ret,
    part,
    ry,
    zsrc,
    zr,
    zres,
    zag,
    ssem,
    rsem,
    cot_sem,
    w_sem,
    cot_ssem,
    w_ssem,
):
    dp = lax.axis_index("dp")
    seq = lax.axis_index("seq")
    z, c = dp // 2, dp % 2
    x, y = seq // 4, seq % 4
    head = 2 * x + c
    own_side = c == y // 2

    def dev(xd, yd, cd):
        return (2 * z + cd, 4 * xd + yd)

    sibling = dev(x, y, 1 - c)

    barrier = pltpu.get_barrier_semaphore()

    def greet(t, carry):
        other = lax.rem(seq + t, 16)
        pl.semaphore_signal(barrier, inc=1, device_id=(2 * z + 1 - c, other), device_id_type=MESH)

        @pl.when(t > 0)
        def _():
            pl.semaphore_signal(barrier, inc=1, device_id=(dp, other), device_id_type=MESH)

        return carry

    lax.fori_loop(0, 16, greet, 0)
    if planes > 1:

        def greet_z(t, carry):
            zd = lax.rem(z + t, planes)
            pl.semaphore_signal(barrier, inc=1, device_id=(2 * zd + c, seq), device_id_type=MESH)
            return carry

        lax.fori_loop(1, planes, greet_z, 0)

    qkv_s[0] = jnp.swapaxes(q_ref[...], 0, 1)
    qkv_s[1] = jnp.swapaxes(k_ref[...], 0, 1)
    qkv_s[2] = jnp.swapaxes(v_ref[...], 0, 1)
    cot_s[...] = jnp.swapaxes(cot_ref[...], 0, 1)

    @pl.when(own_side)
    def _():
        count = count_ref[y % 2]
        key_block = lax.broadcasted_iota(jnp.int32, (8, BLOCK), 0)
        lane = lax.broadcasted_iota(jnp.int32, (8, BLOCK), 1)
        for i in range(8):
            bits = bits_ref[y % 2, i]
            seen = (jnp.right_shift(jnp.full((8, BLOCK), bits, jnp.int32), key_block) & 1) == 1
            limit = jnp.where(seen, count - BLOCK * key_block, 0)
            aux[0:8, i * BLOCK : (i + 1) * BLOCK] = limit.astype(F32)
            live = lane + i * BLOCK < count
            aux[8:16, i * BLOCK : (i + 1) * BLOCK] = jnp.where(live, 1.0, 0.0)

    pl.semaphore_wait(barrier, 31 + planes - 1)

    def push(src, dst, to, s_sem, r_sem):
        same = (to[0] == dp) & (to[1] == seq)

        @pl.when(same)
        def _():
            pltpu.make_async_copy(src, dst, r_sem).start()

        @pl.when(jnp.logical_not(same))
        def _():
            pltpu.make_async_remote_copy(
                src, dst, s_sem, r_sem, device_id=to, device_id_type=MESH
            ).start()

    def send(src, dst, to, s_sem, r_sem):
        pltpu.make_async_remote_copy(
            src, dst, s_sem, r_sem, device_id=to, device_id_type=MESH
        ).start()

    def landed(ref, sem):
        pltpu.make_async_copy(ref, ref, sem).wait()

    @pl.when(own_side)
    def _():
        send(aux, aux, sibling, ssem.at[8], rsem.at[8])

    half = pl.ds(ROWS * (y % 2), ROWS)
    for j in range(2):
        to = dev(x, 2 * c + j, y // 2)
        push(cot_s.at[j], cot_all.at[2 * x + y // 2, half], to, ssem.at[0], rsem.at[0])
    for j in range(2):
        to = dev(x, 2 * c + j, y // 2)
        push(w_ref, w_all.at[2 * x + y // 2, half], to, ssem.at[1], rsem.at[1])

    def send_qkv(t, carry):
        xd = lax.rem(x + t // 4, 4)
        j = lax.rem(t // 2, 2)
        cd = lax.rem(t, 2)
        cols = pl.ds(pl.multiple_of(HEAD * (2 * xd + cd), HEAD), HEAD)
        push(
            qkv_s.at[:, j, :, cols],
            qkv_r.at[:, pl.ds(pl.multiple_of(ROWS * seq, ROWS), ROWS), :],
            dev(xd, 2 * c + j, cd),
            ssem.at[2],
            rsem.at[2],
        )
        return carry

    lax.fori_loop(0, 16, send_qkv, 0)

    right = dev(lax.rem(x + 1, 4), y, c)
    left = dev(lax.rem(x + 3, 4), y, c)
    b_own = head
    b_left = 2 * lax.rem(x + 3, 4) + c
    b_right = 2 * lax.rem(x + 1, 4) + c
    b_far = 2 * lax.rem(x + 2, 4) + c
    low, high = pl.ds(0, ROWS), pl.ds(ROWS, ROWS)

    def ring_first(buf, s, r):
        send(buf.at[b_own], buf.at[b_own], right, s.at[0], r.at[0])
        send(buf.at[b_own], buf.at[b_own], left, s.at[1], r.at[1])
        send(buf.at[b_own], buf.at[b_own], sibling, s.at[2], r.at[2])

    def ring_second(buf, s, r):
        landed(buf.at[b_left], r.at[0])
        send(buf.at[b_left, low], buf.at[b_left, low], right, s.at[4], r.at[4])
        landed(buf.at[b_right], r.at[1])
        send(buf.at[b_right, high], buf.at[b_right, high], left, s.at[6], r.at[6])
        send(buf.at[b_left], buf.at[b_left], sibling, s.at[3], r.at[3])
        send(buf.at[b_right], buf.at[b_right], sibling, s.at[5], r.at[5])

    def ring_third(buf, s, r):
        landed(buf.at[b_far, low], r.at[4])
        send(buf.at[b_far, low], buf.at[b_far, low], sibling, s.at[7], r.at[7])
        landed(buf.at[b_far, high], r.at[6])
        send(buf.at[b_far, high], buf.at[b_far, high], sibling, s.at[8], r.at[8])

    def ring_rest(buf, r):
        other = 1 - 2 * c
        landed(buf.at[b_own + other], r.at[2])
        landed(buf.at[b_left + other], r.at[3])
        landed(buf.at[b_right + other], r.at[5])
        landed(buf.at[b_far + other, low], r.at[7])
        landed(buf.at[b_far + other, high], r.at[8])

    def ring_drain(buf, s):
        for i in (0, 1, 2, 3, 5):
            landed(buf.at[0], s.at[i])
        for i in (4, 6, 7, 8):
            landed(buf.at[0, low], s.at[i])

    landed(cot_all.at[b_own], rsem.at[0])
    ring_first(cot_all, cot_ssem, cot_sem)

    @pl.when(jnp.logical_not(own_side))
    def _():
        landed(aux, rsem.at[8])

    landed(qkv_r, rsem.at[2])

    factor = math.log2(math.e) / math.sqrt(HEAD)
    key_pos = lax.broadcasted_iota(jnp.int32, (BLOCK, IB), 0).astype(F32)
    vt[...] = qkv_r[2].astype(F32).T.astype(BF)
    kt[...] = qkv_r[1].astype(F32).T.astype(BF)

    def forward(i, carry):
        at = pl.multiple_of(i * IB, IB)
        here = pl.ds(at, IB)
        q_part = qkv_r[0, here, :]
        top = jnp.full((8, IB), MASKED, F32)
        for b in range(8):
            rows = pl.ds(b * BLOCK, BLOCK)
            s = lax.dot_general(qkv_r[1, rows, :], q_part, NT, preferred_element_type=F32)
            s = jnp.where(key_pos < aux[b : b + 1, here], s * factor, MASKED)
            scores[rows, :] = s
            top = jnp.maximum(top, jnp.max(s.reshape(BLOCK // 8, 8, IB), axis=0))
        top = jnp.max(top, axis=0, keepdims=True)
        total = jnp.zeros((8, IB), F32)
        for b in range(8):
            rows = pl.ds(b * BLOCK, BLOCK)
            e = jnp.exp2(scores[rows, :] - top)
            scores[rows, :] = e
            total = total + jnp.sum(e.reshape(BLOCK // 8, 8, IB), axis=0)
        inverse = 1.0 / jnp.sum(total, axis=0, keepdims=True)
        for b in range(8):
            rows = pl.ds(b * BLOCK, BLOCK)
            p = scores[rows, :] * inverse
            prob[i, rows, :] = p
            prob_b[rows, here] = p.astype(BF)
        mixed = jnp.dot(vt[...], prob_b[:, here], preferred_element_type=F32)
        mixed = jnp.where(aux[8:9, here] > 0.5, mixed, 0.0)
        att_t[:, here] = mixed.astype(BF)
        att_n[here, :] = mixed.T.astype(BF)
        return carry

    lax.fori_loop(0, 2, forward, 0)
    ring_second(cot_all, cot_ssem, cot_sem)
    landed(w_all.at[b_own], rsem.at[1])
    lax.fori_loop(2, 4, forward, 0)

    my_cols = pl.ds(pl.multiple_of(HEAD * head, HEAD), HEAD)

    def give_back(src, dst, s_sem, r_sem, first, count):
        def one(t, carry):
            to = first + t if count < 16 else lax.rem(seq + t, 16)
            push(
                src.at[pl.ds(pl.multiple_of(ROWS * to, ROWS), ROWS), :],
                dst.at[y % 2, :, my_cols],
                (2 * z + y // 2, to),
                s_sem,
                r_sem,
            )
            return carry

        lax.fori_loop(0, count, one, 0)

    give_back(att_n, att_ret, ssem.at[3], rsem.at[3], 0, 16)

    ring_third(cot_all, cot_ssem, cot_sem)
    ring_rest(cot_all, cot_sem)
    ring_first(w_all, w_ssem, w_sem)

    for b in range(8):
        rows = pl.ds(b * BLOCK, BLOCK)
        g = lax.dot_general(cot_all[b], w_all[b_own], NT, preferred_element_type=F32)
        gt = jnp.where(aux[8:9, b * BLOCK : (b + 1) * BLOCK] > 0.5, g.T, 0.0)
        ag_t[:, rows] = gt.astype(BF)
        ag_n[rows, :] = gt.T.astype(BF)
    part[...] = jnp.dot(
        att_t[...], cot_all[...].reshape(NODES, WIDTH), preferred_element_type=F32
    ).astype(BF)
    for r in range(2):
        for cd in range(2):
            push(
                part.at[pl.ds(ROWS * r, ROWS), pl.ds(512 * cd, 512)],
                ry.at[y],
                dev(x, 2 * c + r, cd),
                ssem.at[7],
                rsem.at[7],
            )

    dqkv_n[2] = jnp.dot(prob_b[...], ag_n[...], preferred_element_type=F32).astype(BF)
    give_back(dqkv_n.at[2], dqkv_ret.at[2], ssem.at[6], rsem.at[6], 0, 16)

    ring_second(w_all, w_ssem, w_sem)

    scale = 1.0 / math.sqrt(HEAD)

    def backward(step, carry):
        i = lax.rem(x + step, 4)
        at = pl.multiple_of(i * IB, IB)
        here = pl.ds(at, IB)
        g_part = ag_n[here, :]
        centre = jnp.sum(
            ag_t[:, here].astype(F32) * att_t[:, here].astype(F32), axis=0, keepdims=True
        )
        for b in range(8):
            rows = pl.ds(b * BLOCK, BLOCK)
            pg = lax.dot_general(qkv_r[2, rows, :], g_part, NT, preferred_element_type=F32)
            sgrad[rows, here] = (prob[i, rows, :] * ((pg - centre) * scale)).astype(BF)
        dq = jnp.dot(kt[...], sgrad[:, here], preferred_element_type=F32)
        dqkv_n[0, here, :] = dq.T.astype(BF)
        give_back(dqkv_n.at[0], dqkv_ret.at[0], ssem.at[4], rsem.at[4], 4 * i, 4)
        return carry

    lax.fori_loop(0, 2, backward, 0)

    landed(ry, rsem.at[7])
    total = ry[0].astype(F32) + ry[1].astype(F32) + ry[2].astype(F32) + ry[3].astype(F32)
    zsrc[...] = total.astype(BF)

    def corner(p, left_edge=0):
        return (
            pl.ds(pl.multiple_of(16 * (p // 4), 16), 16),
            pl.ds(pl.multiple_of(left_edge + 128 * lax.rem(p, 4), 128), 128),
        )

    if planes > 1:

        def send_z(t, carry):
            zd = lax.rem(z + t, planes)
            rows, cols = corner(zd)
            push(
                zsrc.at[rows, cols], zr.at[z], (2 * zd + c, seq), ssem.at[9], rsem.at[9]
            )
            return carry

        lax.fori_loop(0, planes, send_z, 0)

    lax.fori_loop(2, 4, backward, 0)

    dqkv_n[1] = jnp.dot(sgrad[...], qkv_r[0], preferred_element_type=F32).astype(BF)
    give_back(dqkv_n.at[1], dqkv_ret.at[1], ssem.at[5], rsem.at[5], 0, 16)

    my_half = pl.ds(pl.multiple_of(512 * c, 512), 512)
    if planes > 1:
        landed(zr, rsem.at[9])
        zsum = zr[0].astype(F32)
        for p in range(1, planes):
            zsum = zsum + zr[p].astype(F32)
        zres[...] = (zsum * (1.0 / 256.0)).astype(BF)

        def spread(t, carry):
            zd = lax.rem(z + t, planes)
            rows, cols = corner(z, 512 * c)
            push(zres, zag.at[rows, cols], (2 * zd + c, seq), ssem.at[10], rsem.at[10])
            return carry

        lax.fori_loop(0, planes, spread, 0)
    else:
        zag[:, my_half] = (total * (1.0 / 256.0)).astype(BF)

    ring_third(w_all, w_ssem, w_sem)
    landed(att_ret, rsem.at[3])
    ring_rest(w_all, w_sem)
    done = jnp.dot(
        att_ret[...].reshape(2 * ROWS, WIDTH),
        w_all[...].reshape(WIDTH, WIDTH),
        preferred_element_type=F32,
    ).astype(BF)
    done = done.reshape(2, ROWS, WIDTH)
    out_ref[:, 0, :] = done[0]
    out_ref[:, 1, :] = done[1]

    if planes > 1:
        landed(zag.at[:, my_half], rsem.at[10])
    send(zag.at[:, my_half], zag.at[:, my_half], sibling, ssem.at[11], rsem.at[11])

    for i, ref in ((2, dv_ref), (0, dq_ref), (1, dk_ref)):
        landed(dqkv_ret.at[i], rsem.at[4 + i])
        ref[:, 0, :] = dqkv_ret[i, 0]
        ref[:, 1, :] = dqkv_ret[i, 1]

    landed(zag.at[:, pl.ds(pl.multiple_of(512 - 512 * c, 512), 512)], rsem.at[11])
    wg_ref[...] = zag[...].astype(F32)

    def left_here(sem, whole, short, is_short):
        @pl.when(is_short)
        def _():
            landed(short, sem)

        @pl.when(jnp.logical_not(is_short))
        def _():
            landed(whole, sem)

    @pl.when(own_side)
    def _():
        landed(aux, ssem.at[8])

    left_here(ssem.at[0], cot_s, cot_s.at[0], own_side)
    left_here(ssem.at[1], cot_s, cot_s.at[0], own_side)
    most = pl.ds(0, 15 * ROWS)
    left_here(ssem.at[2], qkv_r, qkv_r.at[:, most], own_side)
    left_here(ssem.at[3], att_n, att_n.at[most], own_side)
    for i in range(3):
        left_here(ssem.at[4 + i], dqkv_n.at[i], dqkv_n.at[i, most], own_side)
    left_here(ssem.at[7], ry, ry.at[pl.ds(0, 3)], own_side)
    if planes > 1:
        landed(zr.at[pl.ds(0, planes - 1)], ssem.at[9])
        landed(zr.at[pl.ds(0, planes - 1)], ssem.at[10])
    landed(zag.at[:, my_half], ssem.at[11])
    ring_drain(cot_all, cot_ssem)
    ring_drain(w_all, w_ssem)


def on_device(queries, key_rows, value_rows, cotangent, out_weight, node_counts, edge_bits):
    planes = lax.axis_size("dp") // 2
    vmem = pl.BlockSpec(memory_space=pltpu.VMEM)
    smem = pl.BlockSpec(memory_space=pltpu.SMEM)
    rows3 = jax.ShapeDtypeStruct((ROWS, 2, WIDTH), BF)
    dma = pltpu.SemaphoreType.DMA
    return pl.pallas_call(
        functools.partial(kernel, planes),
        out_shape=(rows3, rows3, rows3, rows3, jax.ShapeDtypeStruct((ROWS, WIDTH), F32)),
        in_specs=[vmem] * 5 + [smem] * 2,
        out_specs=(vmem,) * 5,
        scratch_shapes=[
            pltpu.VMEM((3, 2, ROWS, WIDTH), BF),
            pltpu.VMEM((2, ROWS, WIDTH), BF),
            pltpu.VMEM((3, NODES, HEAD), BF),
            pltpu.VMEM((16, NODES), F32),
            pltpu.VMEM((8, BLOCK, WIDTH), BF),
            pltpu.VMEM((8, BLOCK, WIDTH), BF),
            pltpu.VMEM((NODES, IB), F32),
            pltpu.VMEM((NODES // IB, NODES, IB), F32),
            pltpu.VMEM((NODES, NODES), BF),
            pltpu.VMEM((NODES, NODES), BF),
            pltpu.VMEM((HEAD, NODES), BF),
            pltpu.VMEM((NODES, HEAD), BF),
            pltpu.VMEM((NODES, HEAD), BF),
            pltpu.VMEM((HEAD, NODES), BF),
            pltpu.VMEM((HEAD, NODES), BF),
            pltpu.VMEM((HEAD, NODES), BF),
            pltpu.VMEM((3, NODES, HEAD), BF),
            pltpu.VMEM((2, ROWS, WIDTH), BF),
            pltpu.VMEM((3, 2, ROWS, WIDTH), BF),
            pltpu.VMEM((HEAD, WIDTH), BF),
            pltpu.VMEM((4, ROWS, 512), BF),
            pltpu.VMEM((ROWS, 512), BF),
            pltpu.VMEM((16, 16, 128), BF),
            pltpu.VMEM((16, 128), BF),
            pltpu.VMEM((ROWS, WIDTH), BF),
            dma((12,)),
            dma((12,)),
            dma((9,)),
            dma((9,)),
            dma((9,)),
            dma((9,)),
        ],
        compiler_params=pltpu.CompilerParams(
            collective_id=0, has_side_effects=True, vmem_limit_bytes=48 * 1024 * 1024
        ),
        cost_estimate=pl.CostEstimate(
            flops=3_000_000_000, bytes_accessed=3_000_000, transcendentals=1_000_000
        ),
        name="sublayer",
    )(
        queries,
        key_rows,
        value_rows,
        cotangent,
        out_weight,
        node_counts,
        edge_bits.reshape(2, 8),
    )


def solution(mesh):
    rows = P("seq", "dp", None)
    weight = P("seq", None)
    return jax.shard_map(
        on_device,
        mesh=mesh,
        in_specs=(rows, rows, rows, rows, weight, P("dp"), P("dp", None, None)),
        out_specs=(rows, rows, rows, rows, weight),
        check_vma=False,
    )
```

```python
import functools
import math

import jax
import jax.numpy as jnp
from jax import lax
from jax.experimental import pallas as pl
from jax.experimental.pallas import tpu as pltpu
from jax.sharding import PartitionSpec as P

HEAD = 128
BLOCK = 128
NODES = 1024
WIDTH = 1024
ROWS = 64
IB = 256
MESH = pl.DeviceIdType.MESH
BF = jnp.bfloat16
F32 = jnp.float32
NT = (((1,), (1,)), ((), ()))
MASKED = -1e30


def kernel(
    planes,
    q_ref,
    k_ref,
    v_ref,
    cot_ref,
    w_hbm,
    count_hbm,
    bits_hbm,
    out_ref,
    dq_ref,
    dk_ref,
    dv_ref,
    grad_ref,
    raw,
    w_ref,
    count_ref,
    bits_ref,
    qkv_s,
    cot_s,
    qkv_r,
    aux,
    cot_all,
    w_all,
    scores,
    prob,
    prob_b,
    sgrad,
    att_t,
    att_n,
    ag_n,
    ag_t,
    vt,
    kt,
    dqkv_n,
    att_ret,
    dqkv_ret,
    part,
    ry,
    zsrc,
    zr,
    zres,
    zag,
    mixed_rows,
    wg_f32,
    in_sem,
    out_sem,
    ssem,
    rsem,
    cot_sem,
    w_sem,
    cot_ssem,
    w_ssem,
):
    dp = lax.axis_index("dp")
    seq = lax.axis_index("seq")
    z, c = dp // 2, dp % 2
    x, y = seq // 4, seq % 4
    head = 2 * x + c
    own_side = c == y // 2

    def dev(xd, yd, cd):
        return (2 * z + cd, 4 * xd + yd)

    sibling = dev(x, y, 1 - c)

    incoming = [
        pltpu.make_async_copy(src, dst, in_sem.at[i])
        for i, (src, dst) in enumerate(
            (
                (cot_ref, raw.at[3]),
                (q_ref, raw.at[0]),
                (k_ref, raw.at[1]),
                (v_ref, raw.at[2]),
                (w_hbm, w_ref),
                (count_hbm, count_ref),
                (bits_hbm, bits_ref),
            )
        )
    ]
    for copy in incoming:
        copy.start()

    barrier = pltpu.get_barrier_semaphore()

    def greet(to):
        pl.semaphore_signal(barrier, inc=1, device_id=to, device_id_type=MESH)

    def greet_plane(t, carry):
        xd, j, cd = lax.rem(x + t // 4 + 2, 4), lax.rem(t // 2, 2), lax.rem(t, 2)
        to = dev(xd, 2 * c + j, cd)

        @pl.when(jnp.logical_not((to[0] == dp) & (to[1] == seq)))
        def _():
            greet(to)

        @pl.when(cd == 0)
        def _():
            greet(dev(xd, 2 * (1 - c) + j, y // 2))

        return carry

    def greet_z(t, carry):
        zd = lax.rem(z + t, planes)
        greet((2 * zd, seq))
        greet((2 * zd + 1, seq))
        return carry

    if planes > 1:
        lax.fori_loop(1, planes, greet_z, 0)
    lax.fori_loop(0, 16, greet_plane, 0)

    @pl.when(jnp.logical_not(own_side))
    def _():
        greet(dev(lax.rem(x + 1, 4), y, c))
        greet(dev(lax.rem(x + 3, 4), y, c))

    incoming[0].wait()
    cot_s[...] = jnp.swapaxes(raw[3], 0, 1)
    for i in range(3):
        incoming[1 + i].wait()
        qkv_s[i] = jnp.swapaxes(raw[i], 0, 1)

    @pl.when(own_side)
    def _():
        pl.semaphore_wait(barrier, 23 + 2 * (planes - 1))

    @pl.when(jnp.logical_not(own_side))
    def _():
        pl.semaphore_wait(barrier, 26 + 2 * (planes - 1))

    def push(src, dst, to, s_sem, r_sem):
        same = (to[0] == dp) & (to[1] == seq)

        @pl.when(same)
        def _():
            pltpu.make_async_copy(src, dst, r_sem).start()

        @pl.when(jnp.logical_not(same))
        def _():
            pltpu.make_async_remote_copy(
                src, dst, s_sem, r_sem, device_id=to, device_id_type=MESH
            ).start()

    def send(src, dst, to, s_sem, r_sem):
        pltpu.make_async_remote_copy(
            src, dst, s_sem, r_sem, device_id=to, device_id_type=MESH
        ).start()

    def landed(ref, sem):
        pltpu.make_async_copy(ref, ref, sem).wait()

    half = pl.ds(ROWS * (y % 2), ROWS)
    for j in range(2):
        to = dev(x, 2 * c + j, y // 2)
        push(cot_s.at[j], cot_all.at[2 * x + y // 2, half], to, ssem.at[0], rsem.at[12 + y % 2])

    def send_qkv(first, count, sem):
        def one(t, carry):
            xd, j, cd = lax.rem(x + t // 4 + 2, 4), lax.rem(t // 2, 2), lax.rem(t, 2)
            cols = pl.ds(pl.multiple_of(HEAD * (2 * xd + cd), HEAD), HEAD)
            push(
                qkv_s.at[pl.ds(first, count), j, :, cols],
                qkv_r.at[pl.ds(first, count), pl.ds(pl.multiple_of(ROWS * seq, ROWS), ROWS), :],
                dev(xd, 2 * c + j, cd),
                ssem.at[sem],
                rsem.at[sem],
            )
            return carry

        lax.fori_loop(0, 16, one, 0)

    send_qkv(0, 2, 2)
    send_qkv(2, 1, 9)

    incoming[5].wait()
    incoming[6].wait()

    @pl.when(own_side)
    def _():
        count = count_ref[y % 2]
        key_block = lax.broadcasted_iota(jnp.int32, (8, BLOCK), 0)
        lane = lax.broadcasted_iota(jnp.int32, (8, BLOCK), 1)
        for i in range(8):
            bits = bits_ref[y % 2, i]
            seen = (jnp.right_shift(jnp.full((8, BLOCK), bits, jnp.int32), key_block) & 1) == 1
            limit = jnp.where(seen, count - BLOCK * key_block, 0)
            aux[0:8, i * BLOCK : (i + 1) * BLOCK] = limit.astype(F32)
            live = lane + i * BLOCK < count
            aux[8:16, i * BLOCK : (i + 1) * BLOCK] = jnp.where(live, 1.0, 0.0)
        send(aux, aux, sibling, ssem.at[8], rsem.at[8])

    right = dev(lax.rem(x + 1, 4), y, c)
    left = dev(lax.rem(x + 3, 4), y, c)
    b_own = head
    b_left = 2 * lax.rem(x + 3, 4) + c
    b_right = 2 * lax.rem(x + 1, 4) + c
    b_far = 2 * lax.rem(x + 2, 4) + c
    low, high = pl.ds(0, ROWS), pl.ds(ROWS, ROWS)

    def ring_own(buf, s, r):
        for i, rows, to in (
            (0, low, right),
            (2, high, left),
            (1, high, right),
            (3, low, left),
            (6, low, sibling),
            (7, high, sibling),
        ):
            send(buf.at[b_own, rows], buf.at[b_own, rows], to, s.at[i], r.at[i])

    def ring_forward(buf, s, r):
        landed(buf.at[b_left, low], r.at[0])
        send(buf.at[b_left, low], buf.at[b_left, low], right, s.at[4], r.at[4])
        landed(buf.at[b_right, high], r.at[2])
        send(buf.at[b_right, high], buf.at[b_right, high], left, s.at[5], r.at[5])

    def ring_relay(buf, s, r):
        send(buf.at[b_left, low], buf.at[b_left, low], sibling, s.at[8], r.at[8])
        send(buf.at[b_right, high], buf.at[b_right, high], sibling, s.at[10], r.at[10])
        landed(buf.at[b_left, high], r.at[1])
        send(buf.at[b_left, high], buf.at[b_left, high], sibling, s.at[9], r.at[9])
        landed(buf.at[b_right, low], r.at[3])
        send(buf.at[b_right, low], buf.at[b_right, low], sibling, s.at[11], r.at[11])

    def ring_far(buf, s, r):
        landed(buf.at[b_far, low], r.at[4])
        send(buf.at[b_far, low], buf.at[b_far, low], sibling, s.at[12], r.at[12])
        landed(buf.at[b_far, high], r.at[5])
        send(buf.at[b_far, high], buf.at[b_far, high], sibling, s.at[13], r.at[13])

    def ring_rest(buf, r):
        other = 1 - 2 * c
        for i, b, rows in (
            (6, b_own, low),
            (7, b_own, high),
            (8, b_left, low),
            (9, b_left, high),
            (10, b_right, high),
            (11, b_right, low),
            (12, b_far, low),
            (13, b_far, high),
        ):
            landed(buf.at[b + other, rows], r.at[i])

    def ring_drain(buf, s):
        for i in range(14):
            landed(buf.at[0, low], s.at[i])

    landed(cot_all.at[b_own, low], rsem.at[12])
    landed(cot_all.at[b_own, high], rsem.at[13])
    ring_own(cot_all, cot_ssem, cot_sem)
    ring_forward(cot_all, cot_ssem, cot_sem)

    @pl.when(jnp.logical_not(own_side))
    def _():
        landed(aux, rsem.at[8])

    landed(qkv_r.at[pl.ds(0, 2)], rsem.at[2])

    incoming[4].wait()
    for j in range(2):
        to = dev(x, 2 * c + j, y // 2)
        push(w_ref, w_all.at[2 * x + y // 2, half], to, ssem.at[1], rsem.at[14 + y % 2])

    factor = math.log2(math.e) / math.sqrt(HEAD)
    key_pos = lax.broadcasted_iota(jnp.int32, (BLOCK, IB), 0).astype(F32)

    def forward(i, carry):
        at = pl.multiple_of(i * IB, IB)
        here = pl.ds(at, IB)
        q_part = qkv_r[0, here, :]
        top = jnp.full((8, IB), MASKED, F32)
        for b in range(8):
            rows = pl.ds(b * BLOCK, BLOCK)
            s = lax.dot_general(qkv_r[1, rows, :], q_part, NT, preferred_element_type=F32)
            s = jnp.where(key_pos < aux[b : b + 1, here], s * factor, MASKED)
            scores[rows, :] = s
            top = jnp.maximum(top, jnp.max(s.reshape(BLOCK // 8, 8, IB), axis=0))
        top = jnp.max(top, axis=0, keepdims=True)
        total = jnp.zeros((8, IB), F32)
        for b in range(8):
            rows = pl.ds(b * BLOCK, BLOCK)
            e = jnp.exp2(scores[rows, :] - top)
            scores[rows, :] = e
            total = total + jnp.sum(e.reshape(BLOCK // 8, 8, IB), axis=0)
        inverse = 1.0 / jnp.sum(total, axis=0, keepdims=True)
        for b in range(8):
            rows = pl.ds(b * BLOCK, BLOCK)
            p = scores[rows, :] * inverse
            prob[i, rows, :] = p
            prob_b[rows, here] = p.astype(BF)
        return carry

    lax.fori_loop(0, 4, forward, 0)
    ring_relay(cot_all, cot_ssem, cot_sem)
    kt[...] = qkv_r[1].astype(F32).T.astype(BF)
    landed(qkv_r.at[pl.ds(2, 1)], rsem.at[9])
    vt[...] = qkv_r[2].astype(F32).T.astype(BF)

    def mix(i, carry):
        here = pl.ds(pl.multiple_of(i * IB, IB), IB)
        mixed = jnp.dot(vt[...], prob_b[:, here], preferred_element_type=F32)
        mixed = jnp.where(aux[8:9, here] > 0.5, mixed, 0.0)
        att_t[:, here] = mixed.astype(BF)
        att_n[here, :] = mixed.T.astype(BF)
        return carry

    lax.fori_loop(0, 4, mix, 0)

    my_cols = pl.ds(pl.multiple_of(HEAD * head, HEAD), HEAD)

    def give_back(src, dst, s_sem, r_sem, first, count):
        def one(t, carry):
            to = first + t if count < 16 else lax.rem(seq + t, 16)
            push(
                src.at[pl.ds(pl.multiple_of(ROWS * to, ROWS), ROWS), :],
                dst.at[y % 2, :, my_cols],
                (2 * z + y // 2, to),
                s_sem,
                r_sem,
            )
            return carry

        lax.fori_loop(0, count, one, 0)

    ring_far(cot_all, cot_ssem, cot_sem)
    give_back(att_n, att_ret, ssem.at[3], rsem.at[3], 0, 16)
    ring_rest(cot_all, cot_sem)

    part[...] = jnp.dot(
        att_t[...], cot_all[...].reshape(NODES, WIDTH), preferred_element_type=F32
    ).astype(BF)
    for r in range(2):
        for cd in range(2):
            push(
                part.at[pl.ds(ROWS * r, ROWS), pl.ds(512 * cd, 512)],
                ry.at[y],
                dev(x, 2 * c + r, cd),
                ssem.at[7],
                rsem.at[7],
            )
    landed(w_all.at[b_own, low], rsem.at[14])
    landed(w_all.at[b_own, high], rsem.at[15])
    for b in range(8):
        rows = pl.ds(b * BLOCK, BLOCK)
        g = lax.dot_general(cot_all[b], w_all[b_own], NT, preferred_element_type=F32)
        gt = jnp.where(aux[8:9, b * BLOCK : (b + 1) * BLOCK] > 0.5, g.T, 0.0)
        ag_t[:, rows] = gt.astype(BF)
        ag_n[rows, :] = gt.T.astype(BF)

    dqkv_n[2] = jnp.dot(prob_b[...], ag_n[...], preferred_element_type=F32).astype(BF)
    give_back(dqkv_n.at[2], dqkv_ret.at[2], ssem.at[6], rsem.at[6], 0, 16)

    scale = 1.0 / math.sqrt(HEAD)

    def backward(step, carry):
        i = lax.rem(x + step, 4)
        at = pl.multiple_of(i * IB, IB)
        here = pl.ds(at, IB)
        g_part = ag_n[here, :]
        centre = jnp.sum(
            ag_t[:, here].astype(F32) * att_t[:, here].astype(F32), axis=0, keepdims=True
        )
        for b in range(8):
            rows = pl.ds(b * BLOCK, BLOCK)
            pg = lax.dot_general(qkv_r[2, rows, :], g_part, NT, preferred_element_type=F32)
            sgrad[rows, here] = (prob[i, rows, :] * ((pg - centre) * scale)).astype(BF)
        dq = jnp.dot(kt[...], sgrad[:, here], preferred_element_type=F32)
        dqkv_n[0, here, :] = dq.T.astype(BF)
        give_back(dqkv_n.at[0], dqkv_ret.at[0], ssem.at[4], rsem.at[4], 4 * i, 4)
        return carry

    lax.fori_loop(0, 2, backward, 0)

    landed(ry, rsem.at[7])
    total = ry[0].astype(F32) + ry[1].astype(F32) + ry[2].astype(F32) + ry[3].astype(F32)
    zsrc[...] = total.astype(BF)

    def corner(p, left_edge=0):
        return (
            pl.ds(pl.multiple_of(16 * (p // 4), 16), 16),
            pl.ds(pl.multiple_of(left_edge + 128 * lax.rem(p, 4), 128), 128),
        )

    if planes > 1:

        def send_z(t, carry):
            zd = lax.rem(z + t + planes // 2, planes)
            rows, cols = corner(zd)
            push(zsrc.at[rows, cols], zr.at[z], (2 * zd + c, seq), ssem.at[10], rsem.at[10])
            return carry

        lax.fori_loop(0, planes, send_z, 0)

    lax.fori_loop(2, 4, backward, 0)

    dqkv_n[1] = jnp.dot(sgrad[...], qkv_r[0], preferred_element_type=F32).astype(BF)
    give_back(dqkv_n.at[1], dqkv_ret.at[1], ssem.at[5], rsem.at[5], 0, 16)
    ring_own(w_all, w_ssem, w_sem)

    my_half = pl.ds(pl.multiple_of(512 * c, 512), 512)
    if planes > 1:
        landed(zr, rsem.at[10])
        zsum = zr[0].astype(F32)
        for p in range(1, planes):
            zsum = zsum + zr[p].astype(F32)
        zres[...] = (zsum * (1.0 / 256.0)).astype(BF)

        def spread(t, carry):
            zd = lax.rem(z + t // 2 + planes // 2, planes)
            rows, cols = corner(z, 512 * c)
            to = (2 * zd + lax.rem(t, 2), seq)
            push(zres, zag.at[rows, cols], to, ssem.at[11], rsem.at[11])
            return carry

        lax.fori_loop(0, 2 * planes, spread, 0)
    else:
        zag[:, my_half] = (total * (1.0 / 256.0)).astype(BF)
        send(zag.at[:, my_half], zag.at[:, my_half], sibling, ssem.at[11], rsem.at[11])

    ring_forward(w_all, w_ssem, w_sem)
    ring_relay(w_all, w_ssem, w_sem)
    ring_far(w_all, w_ssem, w_sem)
    landed(att_ret, rsem.at[3])
    ring_rest(w_all, w_sem)
    done = jnp.dot(
        att_ret[...].reshape(2 * ROWS, WIDTH),
        w_all[...].reshape(WIDTH, WIDTH),
        preferred_element_type=F32,
    ).astype(BF)
    outgoing = []

    def write(i, src, dst):
        outgoing.append(pltpu.make_async_copy(src, dst, out_sem.at[i]))
        outgoing[-1].start()

    mixed_rows[3] = jnp.swapaxes(done.reshape(2, ROWS, WIDTH), 0, 1)
    write(3, mixed_rows.at[3], out_ref)
    for i, ref in ((2, dv_ref), (0, dq_ref), (1, dk_ref)):
        landed(dqkv_ret.at[i], rsem.at[4 + i])
        mixed_rows[i] = jnp.swapaxes(dqkv_ret[i], 0, 1)
        write(i, mixed_rows.at[i], ref)

    if planes > 1:
        landed(zag, rsem.at[11])
    else:
        landed(zag.at[:, pl.ds(pl.multiple_of(512 - 512 * c, 512), 512)], rsem.at[11])
    wg_f32[...] = zag[...].astype(F32)
    write(4, wg_f32, grad_ref)

    def left_here(sem, whole, short, is_short):
        @pl.when(is_short)
        def _():
            landed(short, sem)

        @pl.when(jnp.logical_not(is_short))
        def _():
            landed(whole, sem)

    @pl.when(own_side)
    def _():
        landed(aux, ssem.at[8])

    left_here(ssem.at[0], cot_s, cot_s.at[0], own_side)
    left_here(ssem.at[1], cot_s, cot_s.at[0], own_side)
    most = pl.ds(0, 15 * ROWS)
    left_here(ssem.at[2], qkv_r.at[0:2], qkv_r.at[0:2, most], own_side)
    left_here(ssem.at[9], qkv_r.at[2], qkv_r.at[2, most], own_side)
    left_here(ssem.at[3], att_n, att_n.at[most], own_side)
    for i in range(3):
        left_here(ssem.at[4 + i], dqkv_n.at[i], dqkv_n.at[i, most], own_side)
    left_here(ssem.at[7], ry, ry.at[pl.ds(0, 3)], own_side)
    if planes > 1:
        landed(zr.at[pl.ds(0, planes - 1)], ssem.at[10])
        landed(zr.at[pl.ds(0, planes - 1)], ssem.at[11])
        landed(zr, ssem.at[11])
    else:
        landed(zag.at[:, my_half], ssem.at[11])
    ring_drain(cot_all, cot_ssem)
    ring_drain(w_all, w_ssem)
    for copy in outgoing:
        copy.wait()


def finish(*refs):
    sem = refs[-1]
    copies = [pltpu.make_async_copy(refs[i], refs[5 + i], sem.at[i]) for i in range(5)]
    for copy in copies:
        copy.start()
    for copy in copies:
        copy.wait()


def on_device(queries, key_rows, value_rows, cotangent, out_weight, node_counts, edge_bits):
    planes = lax.axis_size("dp") // 2
    hbm = pl.BlockSpec(memory_space=pltpu.HBM)
    most_vmem = 60 * 1024 * 1024
    rows3 = jax.ShapeDtypeStruct((ROWS, 2, WIDTH), BF)
    grad = jax.ShapeDtypeStruct((ROWS, WIDTH), F32)
    dma = pltpu.SemaphoreType.DMA
    shapes = (rows3, rows3, rows3, rows3, grad)
    results = pl.pallas_call(
        functools.partial(kernel, planes),
        out_shape=shapes,
        in_specs=[hbm] * 7,
        out_specs=(hbm,) * 5,
        scratch_shapes=[
            pltpu.VMEM((4, ROWS, 2, WIDTH), BF),
            pltpu.VMEM((ROWS, WIDTH), BF),
            pltpu.SMEM((2,), jnp.int32),
            pltpu.SMEM((2, 8), jnp.int32),
            pltpu.VMEM((3, 2, ROWS, WIDTH), BF),
            pltpu.VMEM((2, ROWS, WIDTH), BF),
            pltpu.VMEM((3, NODES, HEAD), BF),
            pltpu.VMEM((16, NODES), F32),
            pltpu.VMEM((8, BLOCK, WIDTH), BF),
            pltpu.VMEM((8, BLOCK, WIDTH), BF),
            pltpu.VMEM((NODES, IB), F32),
            pltpu.VMEM((NODES // IB, NODES, IB), F32),
            pltpu.VMEM((NODES, NODES), BF),
            pltpu.VMEM((NODES, NODES), BF),
            pltpu.VMEM((HEAD, NODES), BF),
            pltpu.VMEM((NODES, HEAD), BF),
            pltpu.VMEM((NODES, HEAD), BF),
            pltpu.VMEM((HEAD, NODES), BF),
            pltpu.VMEM((HEAD, NODES), BF),
            pltpu.VMEM((HEAD, NODES), BF),
            pltpu.VMEM((3, NODES, HEAD), BF),
            pltpu.VMEM((2, ROWS, WIDTH), BF),
            pltpu.VMEM((3, 2, ROWS, WIDTH), BF),
            pltpu.VMEM((HEAD, WIDTH), BF),
            pltpu.VMEM((4, ROWS, 512), BF),
            pltpu.VMEM((ROWS, 512), BF),
            pltpu.VMEM((16, 16, 128), BF),
            pltpu.VMEM((16, 128), BF),
            pltpu.VMEM((ROWS, WIDTH), BF),
            pltpu.VMEM((4, ROWS, 2, WIDTH), BF),
            pltpu.VMEM((ROWS, WIDTH), F32),
            dma((7,)),
            dma((5,)),
            dma((12,)),
            dma((16,)),
            dma((14,)),
            dma((14,)),
            dma((14,)),
            dma((14,)),
        ],
        compiler_params=pltpu.CompilerParams(
            collective_id=0, has_side_effects=True, vmem_limit_bytes=most_vmem
        ),
        cost_estimate=pl.CostEstimate(
            flops=3_000_000_000, bytes_accessed=3_000_000, transcendentals=1_000_000
        ),
        name="sublayer",
    )(
        queries,
        key_rows,
        value_rows,
        cotangent,
        out_weight,
        node_counts,
        edge_bits.reshape(2, 8),
    )
    return pl.pallas_call(
        finish,
        out_shape=shapes,
        in_specs=[hbm] * 5,
        out_specs=(hbm,) * 5,
        scratch_shapes=[dma((5,))],
        compiler_params=pltpu.CompilerParams(vmem_limit_bytes=most_vmem),
        name="results",
    )(*results)


def solution(mesh):
    rows = P("seq", "dp", None)
    weight = P("seq", None)
    return jax.shard_map(
        on_device,
        mesh=mesh,
        in_specs=(rows, rows, rows, rows, weight, P("dp"), P("dp", None, None)),
        out_specs=(rows, rows, rows, rows, weight),
        check_vma=False,
    )
```

```python
import functools
import math

import jax
import jax.numpy as jnp
from jax import lax
from jax.experimental import pallas as pl
from jax.experimental.pallas import tpu as pltpu
from jax.sharding import PartitionSpec as P

HEAD = 128
BLOCK = 128
NODES = 1024
WIDTH = 1024
ROWS = 64
IB = 256
MESH = pl.DeviceIdType.MESH
BF = jnp.bfloat16
F32 = jnp.float32
NT = (((1,), (1,)), ((), ()))
MASKED = -1e30


def kernel(
    planes,
    q_ref,
    k_ref,
    v_ref,
    cot_ref,
    w_hbm,
    count_hbm,
    bits_hbm,
    out_ref,
    dq_ref,
    dk_ref,
    dv_ref,
    grad_ref,
    raw,
    w_ref,
    count_ref,
    bits_ref,
    qkv_s,
    cot_s,
    qkv_r,
    aux,
    cot_all,
    w_all,
    scores,
    prob,
    prob_b,
    sgrad,
    att_t,
    att_n,
    ag_n,
    ag_t,
    vt,
    kt,
    dqkv_n,
    att_ret,
    dqkv_ret,
    part,
    ry,
    zsrc,
    zr,
    zres,
    zag,
    mixed_rows,
    wg_f32,
    in_sem,
    out_sem,
    ssem,
    rsem,
    cot_sem,
    w_sem,
    cot_ssem,
    w_ssem,
):
    dp = lax.axis_index("dp")
    seq = lax.axis_index("seq")
    z, c = dp // 2, dp % 2
    x, y = seq // 4, seq % 4
    head = 2 * x + c
    own_side = c == y // 2

    def dev(xd, yd, cd):
        return (2 * z + cd, 4 * xd + yd)

    sibling = dev(x, y, 1 - c)

    incoming = [
        pltpu.make_async_copy(src, dst, in_sem.at[i])
        for i, (src, dst) in enumerate(
            (
                (cot_ref, raw.at[3]),
                (q_ref, raw.at[0]),
                (k_ref, raw.at[1]),
                (v_ref, raw.at[2]),
                (w_hbm, w_ref),
                (count_hbm, count_ref),
                (bits_hbm, bits_ref),
            )
        )
    ]
    for copy in incoming:
        copy.start()

    barrier = pltpu.get_barrier_semaphore()

    def greet(to):
        pl.semaphore_signal(barrier, inc=1, device_id=to, device_id_type=MESH)

    def greet_plane(t, carry):
        xd, j, cd = lax.rem(x + t // 4 + 2, 4), lax.rem(t // 2, 2), lax.rem(t, 2)
        to = dev(xd, 2 * c + j, cd)

        @pl.when(jnp.logical_not((to[0] == dp) & (to[1] == seq)))
        def _():
            greet(to)

        @pl.when(cd == 0)
        def _():
            greet(dev(xd, 2 * (1 - c) + j, y // 2))

        return carry

    def greet_z(t, carry):
        zd = lax.rem(z + t, planes)
        greet((2 * zd + c, seq))
        return carry

    if planes > 1:
        lax.fori_loop(1, planes, greet_z, 0)
    lax.fori_loop(0, 16, greet_plane, 0)

    @pl.when(jnp.logical_not(own_side))
    def _():
        greet(dev(lax.rem(x + 1, 4), y, c))
        greet(dev(lax.rem(x + 3, 4), y, c))

    incoming[0].wait()
    cot_s[...] = jnp.swapaxes(raw[3], 0, 1)
    for i in range(3):
        incoming[1 + i].wait()
        qkv_s[i] = jnp.swapaxes(raw[i], 0, 1)

    @pl.when(own_side)
    def _():
        pl.semaphore_wait(barrier, 23 + planes - 1)

    @pl.when(jnp.logical_not(own_side))
    def _():
        pl.semaphore_wait(barrier, 26 + planes - 1)

    def push(src, dst, to, s_sem, r_sem):
        same = (to[0] == dp) & (to[1] == seq)

        @pl.when(same)
        def _():
            pltpu.make_async_copy(src, dst, r_sem).start()

        @pl.when(jnp.logical_not(same))
        def _():
            pltpu.make_async_remote_copy(
                src, dst, s_sem, r_sem, device_id=to, device_id_type=MESH
            ).start()

    def send(src, dst, to, s_sem, r_sem):
        pltpu.make_async_remote_copy(
            src, dst, s_sem, r_sem, device_id=to, device_id_type=MESH
        ).start()

    def landed(ref, sem):
        pltpu.make_async_copy(ref, ref, sem).wait()

    half = pl.ds(ROWS * (y % 2), ROWS)
    for j in range(2):
        to = dev(x, 2 * c + j, y // 2)
        push(cot_s.at[j], cot_all.at[2 * x + y // 2, half], to, ssem.at[0], rsem.at[12 + y % 2])

    def send_qkv(first, count, sem):
        def one(t, carry):
            xd, j, cd = lax.rem(x + t // 4 + 2, 4), lax.rem(t // 2, 2), lax.rem(t, 2)
            cols = pl.ds(pl.multiple_of(HEAD * (2 * xd + cd), HEAD), HEAD)
            push(
                qkv_s.at[pl.ds(first, count), j, :, cols],
                qkv_r.at[pl.ds(first, count), pl.ds(pl.multiple_of(ROWS * seq, ROWS), ROWS), :],
                dev(xd, 2 * c + j, cd),
                ssem.at[sem],
                rsem.at[sem],
            )
            return carry

        lax.fori_loop(0, 16, one, 0)

    send_qkv(0, 2, 2)
    send_qkv(2, 1, 9)

    incoming[5].wait()
    incoming[6].wait()

    @pl.when(own_side)
    def _():
        count = count_ref[y % 2]
        key_block = lax.broadcasted_iota(jnp.int32, (8, BLOCK), 0)
        lane = lax.broadcasted_iota(jnp.int32, (8, BLOCK), 1)
        for i in range(8):
            bits = bits_ref[y % 2, i]
            seen = (jnp.right_shift(jnp.full((8, BLOCK), bits, jnp.int32), key_block) & 1) == 1
            limit = jnp.where(seen, count - BLOCK * key_block, 0)
            aux[0:8, i * BLOCK : (i + 1) * BLOCK] = limit.astype(F32)
            live = lane + i * BLOCK < count
            aux[8:16, i * BLOCK : (i + 1) * BLOCK] = jnp.where(live, 1.0, 0.0)
        send(aux, aux, sibling, ssem.at[8], rsem.at[8])

    right = dev(lax.rem(x + 1, 4), y, c)
    left = dev(lax.rem(x + 3, 4), y, c)
    b_own = head
    b_left = 2 * lax.rem(x + 3, 4) + c
    b_right = 2 * lax.rem(x + 1, 4) + c
    b_far = 2 * lax.rem(x + 2, 4) + c
    low, high = pl.ds(0, ROWS), pl.ds(ROWS, ROWS)

    def ring_own(buf, s, r):
        for i, rows, to in (
            (0, low, right),
            (2, high, left),
            (1, high, right),
            (3, low, left),
            (6, low, sibling),
            (7, high, sibling),
        ):
            send(buf.at[b_own, rows], buf.at[b_own, rows], to, s.at[i], r.at[i])

    def ring_forward(buf, s, r):
        landed(buf.at[b_left, low], r.at[0])
        send(buf.at[b_left, low], buf.at[b_left, low], right, s.at[4], r.at[4])
        landed(buf.at[b_right, high], r.at[2])
        send(buf.at[b_right, high], buf.at[b_right, high], left, s.at[5], r.at[5])

    def ring_relay(buf, s, r):
        send(buf.at[b_left, low], buf.at[b_left, low], sibling, s.at[8], r.at[8])
        send(buf.at[b_right, high], buf.at[b_right, high], sibling, s.at[10], r.at[10])
        landed(buf.at[b_left, high], r.at[1])
        send(buf.at[b_left, high], buf.at[b_left, high], sibling, s.at[9], r.at[9])
        landed(buf.at[b_right, low], r.at[3])
        send(buf.at[b_right, low], buf.at[b_right, low], sibling, s.at[11], r.at[11])

    def ring_far(buf, s, r):
        landed(buf.at[b_far, low], r.at[4])
        send(buf.at[b_far, low], buf.at[b_far, low], sibling, s.at[12], r.at[12])
        landed(buf.at[b_far, high], r.at[5])
        send(buf.at[b_far, high], buf.at[b_far, high], sibling, s.at[13], r.at[13])

    def ring_rest(buf, r):
        other = 1 - 2 * c
        for i, b, rows in (
            (6, b_own, low),
            (7, b_own, high),
            (8, b_left, low),
            (9, b_left, high),
            (10, b_right, high),
            (11, b_right, low),
            (12, b_far, low),
            (13, b_far, high),
        ):
            landed(buf.at[b + other, rows], r.at[i])

    def ring_drain(buf, s):
        for i in range(14):
            landed(buf.at[0, low], s.at[i])

    landed(cot_all.at[b_own, low], rsem.at[12])
    landed(cot_all.at[b_own, high], rsem.at[13])
    ring_own(cot_all, cot_ssem, cot_sem)
    ring_forward(cot_all, cot_ssem, cot_sem)

    @pl.when(jnp.logical_not(own_side))
    def _():
        landed(aux, rsem.at[8])

    landed(qkv_r.at[pl.ds(0, 2)], rsem.at[2])

    incoming[4].wait()
    for j in range(2):
        to = dev(x, 2 * c + j, y // 2)
        push(w_ref, w_all.at[2 * x + y // 2, half], to, ssem.at[1], rsem.at[14 + y % 2])

    factor = math.log2(math.e) / math.sqrt(HEAD)
    key_pos = lax.broadcasted_iota(jnp.int32, (BLOCK, IB), 0).astype(F32)

    def forward(i, carry):
        at = pl.multiple_of(i * IB, IB)
        here = pl.ds(at, IB)
        q_part = qkv_r[0, here, :]
        top = jnp.full((8, IB), MASKED, F32)
        for b in range(8):
            rows = pl.ds(b * BLOCK, BLOCK)
            s = lax.dot_general(qkv_r[1, rows, :], q_part, NT, preferred_element_type=F32)
            s = jnp.where(key_pos < aux[b : b + 1, here], s * factor, MASKED)
            scores[rows, :] = s
            top = jnp.maximum(top, jnp.max(s.reshape(BLOCK // 8, 8, IB), axis=0))
        top = jnp.max(top, axis=0, keepdims=True)
        total = jnp.zeros((8, IB), F32)
        for b in range(8):
            rows = pl.ds(b * BLOCK, BLOCK)
            e = jnp.exp2(scores[rows, :] - top)
            scores[rows, :] = e
            total = total + jnp.sum(e.reshape(BLOCK // 8, 8, IB), axis=0)
        inverse = 1.0 / jnp.sum(total, axis=0, keepdims=True)
        for b in range(8):
            rows = pl.ds(b * BLOCK, BLOCK)
            p = scores[rows, :] * inverse
            prob[i, rows, :] = p
            prob_b[rows, here] = p.astype(BF)
        return carry

    lax.fori_loop(0, 4, forward, 0)
    ring_relay(cot_all, cot_ssem, cot_sem)
    kt[...] = qkv_r[1].astype(F32).T.astype(BF)
    landed(qkv_r.at[pl.ds(2, 1)], rsem.at[9])
    vt[...] = qkv_r[2].astype(F32).T.astype(BF)

    def mix(i, carry):
        here = pl.ds(pl.multiple_of(i * IB, IB), IB)
        mixed = jnp.dot(vt[...], prob_b[:, here], preferred_element_type=F32)
        mixed = jnp.where(aux[8:9, here] > 0.5, mixed, 0.0)
        att_t[:, here] = mixed.astype(BF)
        att_n[here, :] = mixed.T.astype(BF)
        return carry

    lax.fori_loop(0, 4, mix, 0)

    my_cols = pl.ds(pl.multiple_of(HEAD * head, HEAD), HEAD)

    def give_back(src, dst, s_sem, r_sem, first, count):
        def one(t, carry):
            to = first + t if count < 16 else lax.rem(seq + t, 16)
            push(
                src.at[pl.ds(pl.multiple_of(ROWS * to, ROWS), ROWS), :],
                dst.at[y % 2, :, my_cols],
                (2 * z + y // 2, to),
                s_sem,
                r_sem,
            )
            return carry

        lax.fori_loop(0, count, one, 0)

    ring_far(cot_all, cot_ssem, cot_sem)
    give_back(att_n, att_ret, ssem.at[3], rsem.at[3], 0, 16)
    ring_rest(cot_all, cot_sem)

    cot_rows = cot_all[...].reshape(NODES, WIDTH)
    for h in range(2):
        for cd in range(2):
            edge = 512 * cd + 256 * h
            part[:, edge : edge + 256] = jnp.dot(
                att_t[...], cot_rows[:, edge : edge + 256], preferred_element_type=F32
            ).astype(BF)
            for r in range(2):
                push(
                    part.at[pl.ds(ROWS * r, ROWS), pl.ds(edge, 256)],
                    ry.at[h, y],
                    dev(x, 2 * c + r, cd),
                    ssem.at[7],
                    rsem.at[7 if h == 0 else 10],
                )
    landed(w_all.at[b_own, low], rsem.at[14])
    landed(w_all.at[b_own, high], rsem.at[15])
    ring_own(w_all, w_ssem, w_sem)
    for b in range(8):
        rows = pl.ds(b * BLOCK, BLOCK)
        g = lax.dot_general(cot_all[b], w_all[b_own], NT, preferred_element_type=F32)
        gt = jnp.where(aux[8:9, b * BLOCK : (b + 1) * BLOCK] > 0.5, g.T, 0.0)
        ag_t[:, rows] = gt.astype(BF)
        ag_n[rows, :] = gt.T.astype(BF)

    dqkv_n[2] = jnp.dot(prob_b[...], ag_n[...], preferred_element_type=F32).astype(BF)
    give_back(dqkv_n.at[2], dqkv_ret.at[2], ssem.at[6], rsem.at[6], 0, 16)

    scale = 1.0 / math.sqrt(HEAD)

    def backward(step, carry):
        i = lax.rem(x + step, 4)
        at = pl.multiple_of(i * IB, IB)
        here = pl.ds(at, IB)
        g_part = ag_n[here, :]
        centre = jnp.sum(
            ag_t[:, here].astype(F32) * att_t[:, here].astype(F32), axis=0, keepdims=True
        )
        for b in range(8):
            rows = pl.ds(b * BLOCK, BLOCK)
            pg = lax.dot_general(qkv_r[2, rows, :], g_part, NT, preferred_element_type=F32)
            sgrad[rows, here] = (prob[i, rows, :] * ((pg - centre) * scale)).astype(BF)
        dq = jnp.dot(kt[...], sgrad[:, here], preferred_element_type=F32)
        dqkv_n[0, here, :] = dq.T.astype(BF)
        give_back(dqkv_n.at[0], dqkv_ret.at[0], ssem.at[4], rsem.at[4], 4 * i, 4)
        return carry

    def corner(p, edge):
        q = p // 2
        return (
            pl.ds(pl.multiple_of(16 * lax.rem(q, 4), 16), 16),
            pl.ds(pl.multiple_of(edge + 128 * (q // 4), 128), 128),
        )

    def to_planes(h):
        landed(ry.at[h], rsem.at[7 if h == 0 else 10])
        total = ry[h, 0].astype(F32) + ry[h, 1].astype(F32)
        total = total + ry[h, 2].astype(F32) + ry[h, 3].astype(F32)
        zsrc[h] = total.astype(BF)
        if planes == 1:
            zag[:, pl.ds(pl.multiple_of(512 * c + 256 * h, 256), 256)] = (
                total * (1.0 / 256.0)
            ).astype(BF)
            return

        def send_z(t, carry):
            zd = 2 * lax.rem(z // 2 + t + 4, planes // 2) + h
            rows, cols = corner(zd, 0)
            push(zsrc.at[h, rows, cols], zr.at[z], (2 * zd + c, seq), ssem.at[10], rsem.at[16])
            return carry

        lax.fori_loop(0, planes // 2, send_z, 0)

    lax.fori_loop(0, 1, backward, 0)
    to_planes(0)
    lax.fori_loop(1, 2, backward, 0)
    to_planes(1)
    lax.fori_loop(2, 4, backward, 0)
    dqkv_n[1] = jnp.dot(sgrad[...], qkv_r[0], preferred_element_type=F32).astype(BF)
    give_back(dqkv_n.at[1], dqkv_ret.at[1], ssem.at[5], rsem.at[5], 0, 16)
    ring_forward(w_all, w_ssem, w_sem)
    ring_relay(w_all, w_ssem, w_sem)

    if planes > 1:
        landed(zr, rsem.at[16])
        zsum = zr[0].astype(F32)
        for p in range(1, planes):
            zsum = zsum + zr[p].astype(F32)
        zres[...] = (zsum * (1.0 / 256.0)).astype(BF)
        parity = lax.rem(z, 2)
        rows, cols = corner(z, 512 * c + 256 * parity)

        def spread(t, carry):
            zd = lax.rem(z + t + planes // 2, planes)
            to = (2 * zd + c, seq)
            push(zres, zag.at[rows, cols], to, ssem.at[11], rsem.at[17 + parity])
            return carry

        lax.fori_loop(0, planes, spread, 0)

    ring_far(w_all, w_ssem, w_sem)
    landed(att_ret, rsem.at[3])
    ring_rest(w_all, w_sem)
    done = jnp.dot(
        att_ret[...].reshape(2 * ROWS, WIDTH),
        w_all[...].reshape(WIDTH, WIDTH),
        preferred_element_type=F32,
    ).astype(BF)
    outgoing = []

    def write(i, src, dst):
        outgoing.append(pltpu.make_async_copy(src, dst, out_sem.at[i]))
        outgoing[-1].start()

    mixed_rows[3] = jnp.swapaxes(done.reshape(2, ROWS, WIDTH), 0, 1)
    write(3, mixed_rows.at[3], out_ref)
    for i, ref in ((2, dv_ref), (0, dq_ref), (1, dk_ref)):
        landed(dqkv_ret.at[i], rsem.at[4 + i])
        mixed_rows[i] = jnp.swapaxes(dqkv_ret[i], 0, 1)
        write(i, mixed_rows.at[i], ref)

    for h in range(2):
        mine = zag.at[:, pl.ds(pl.multiple_of(512 * c + 256 * h, 256), 256)]
        if planes > 1:
            landed(mine, rsem.at[17 + h])
        send(mine, mine, sibling, ssem.at[12 + h], rsem.at[19 + h])
    for h in range(2):
        landed(zag.at[:, pl.ds(pl.multiple_of(512 - 512 * c + 256 * h, 256), 256)], rsem.at[19 + h])
    wg_f32[...] = zag[...].astype(F32)
    write(4, wg_f32, grad_ref)

    def left_here(sem, whole, short, is_short):
        @pl.when(is_short)
        def _():
            landed(short, sem)

        @pl.when(jnp.logical_not(is_short))
        def _():
            landed(whole, sem)

    @pl.when(own_side)
    def _():
        landed(aux, ssem.at[8])

    left_here(ssem.at[0], cot_s, cot_s.at[0], own_side)
    left_here(ssem.at[1], cot_s, cot_s.at[0], own_side)
    most = pl.ds(0, 15 * ROWS)
    left_here(ssem.at[2], qkv_r.at[0:2], qkv_r.at[0:2, most], own_side)
    left_here(ssem.at[9], qkv_r.at[2], qkv_r.at[2, most], own_side)
    left_here(ssem.at[3], att_n, att_n.at[most], own_side)
    for i in range(3):
        left_here(ssem.at[4 + i], dqkv_n.at[i], dqkv_n.at[i, most], own_side)
    left_here(ssem.at[7], ry, ry.at[:, pl.ds(0, 3)], own_side)
    if planes > 1:
        landed(zr.at[pl.ds(0, planes - 1)], ssem.at[10])
        landed(zr.at[pl.ds(0, planes - 1)], ssem.at[11])
    for h in range(2):
        landed(zag.at[:, pl.ds(256 * h, 256)], ssem.at[12 + h])
    ring_drain(cot_all, cot_ssem)
    ring_drain(w_all, w_ssem)
    for copy in outgoing:
        copy.wait()


def finish(*refs):
    held, sem = refs[10:15], refs[15]
    inward = [pltpu.make_async_copy(refs[i], held[i], sem.at[i]) for i in range(5)]
    outward = [pltpu.make_async_copy(held[i], refs[5 + i], sem.at[5 + i]) for i in range(5)]
    for copy in inward:
        copy.start()
    for first, second in zip(inward, outward):
        first.wait()
        second.start()
    for copy in outward:
        copy.wait()


def on_device(queries, key_rows, value_rows, cotangent, out_weight, node_counts, edge_bits):
    planes = lax.axis_size("dp") // 2
    hbm = pl.BlockSpec(memory_space=pltpu.HBM)
    most_vmem = 60 * 1024 * 1024
    rows3 = jax.ShapeDtypeStruct((ROWS, 2, WIDTH), BF)
    grad = jax.ShapeDtypeStruct((ROWS, WIDTH), F32)
    dma = pltpu.SemaphoreType.DMA
    shapes = (rows3, rows3, rows3, rows3, grad)
    results = pl.pallas_call(
        functools.partial(kernel, planes),
        out_shape=shapes,
        in_specs=[hbm] * 7,
        out_specs=(hbm,) * 5,
        scratch_shapes=[
            pltpu.VMEM((4, ROWS, 2, WIDTH), BF),
            pltpu.VMEM((ROWS, WIDTH), BF),
            pltpu.SMEM((2,), jnp.int32),
            pltpu.SMEM((2, 8), jnp.int32),
            pltpu.VMEM((3, 2, ROWS, WIDTH), BF),
            pltpu.VMEM((2, ROWS, WIDTH), BF),
            pltpu.VMEM((3, NODES, HEAD), BF),
            pltpu.VMEM((16, NODES), F32),
            pltpu.VMEM((8, BLOCK, WIDTH), BF),
            pltpu.VMEM((8, BLOCK, WIDTH), BF),
            pltpu.VMEM((NODES, IB), F32),
            pltpu.VMEM((NODES // IB, NODES, IB), F32),
            pltpu.VMEM((NODES, NODES), BF),
            pltpu.VMEM((NODES, NODES), BF),
            pltpu.VMEM((HEAD, NODES), BF),
            pltpu.VMEM((NODES, HEAD), BF),
            pltpu.VMEM((NODES, HEAD), BF),
            pltpu.VMEM((HEAD, NODES), BF),
            pltpu.VMEM((HEAD, NODES), BF),
            pltpu.VMEM((HEAD, NODES), BF),
            pltpu.VMEM((3, NODES, HEAD), BF),
            pltpu.VMEM((2, ROWS, WIDTH), BF),
            pltpu.VMEM((3, 2, ROWS, WIDTH), BF),
            pltpu.VMEM((HEAD, WIDTH), BF),
            pltpu.VMEM((2, 4, ROWS, 256), BF),
            pltpu.VMEM((2, ROWS, 256), BF),
            pltpu.VMEM((16, 16, 128), BF),
            pltpu.VMEM((16, 128), BF),
            pltpu.VMEM((ROWS, WIDTH), BF),
            pltpu.VMEM((4, ROWS, 2, WIDTH), BF),
            pltpu.VMEM((ROWS, WIDTH), F32),
            dma((7,)),
            dma((5,)),
            dma((14,)),
            dma((21,)),
            dma((14,)),
            dma((14,)),
            dma((14,)),
            dma((14,)),
        ],
        compiler_params=pltpu.CompilerParams(
            collective_id=0, has_side_effects=True, vmem_limit_bytes=most_vmem
        ),
        cost_estimate=pl.CostEstimate(
            flops=3_000_000_000, bytes_accessed=3_000_000, transcendentals=1_000_000
        ),
        name="sublayer",
    )(
        queries,
        key_rows,
        value_rows,
        cotangent,
        out_weight,
        node_counts,
        edge_bits.reshape(2, 8),
    )
    return pl.pallas_call(
        finish,
        out_shape=shapes,
        in_specs=[hbm] * 5,
        out_specs=(hbm,) * 5,
        scratch_shapes=[pltpu.VMEM(one.shape, one.dtype) for one in shapes] + [dma((10,))],
        compiler_params=pltpu.CompilerParams(vmem_limit_bytes=most_vmem),
        name="results",
    )(*results)


def solution(mesh):
    rows = P("seq", "dp", None)
    weight = P("seq", None)
    return jax.shard_map(
        on_device,
        mesh=mesh,
        in_specs=(rows, rows, rows, rows, weight, P("dp"), P("dp", None, None)),
        out_specs=(rows, rows, rows, rows, weight),
        check_vma=False,
    )
```

```python
import functools
import math

import jax
import jax.numpy as jnp
from jax import lax
from jax.experimental import pallas as pl
from jax.experimental.pallas import tpu as pltpu
from jax.sharding import PartitionSpec as P

HEAD = 128
BLOCK = 128
NODES = 1024
WIDTH = 1024
ROWS = 64
IB = 256
MESH = pl.DeviceIdType.MESH
BF = jnp.bfloat16
F32 = jnp.float32
NT = (((1,), (1,)), ((), ()))
MASKED = -1e30


def kernel(
    planes,
    q_ref,
    k_ref,
    v_ref,
    cot_ref,
    w_hbm,
    count_hbm,
    bits_hbm,
    out_ref,
    dq_ref,
    dk_ref,
    dv_ref,
    grad_ref,
    raw,
    w_ref,
    count_ref,
    bits_ref,
    qkv_s,
    cot_s,
    qkv_r,
    aux,
    cot_all,
    w_all,
    scores,
    prob,
    prob_b,
    sgrad,
    att_t,
    att_n,
    ag_n,
    ag_t,
    vt,
    kt,
    dqkv_n,
    att_ret,
    dqkv_ret,
    part,
    ry,
    zsrc,
    zr,
    zres,
    zag,
    mixed_rows,
    wg_f32,
    in_sem,
    out_sem,
    ssem,
    rsem,
    cot_sem,
    w_sem,
    cot_ssem,
    w_ssem,
    known,
):
    dp = lax.axis_index("dp")
    seq = lax.axis_index("seq")
    z, c = dp // 2, dp % 2
    x, y = seq // 4, seq % 4
    head = 2 * x + c
    own_side = c == y // 2

    def dev(xd, yd, cd):
        return (2 * z + cd, 4 * xd + yd)

    sibling = dev(x, y, 1 - c)

    incoming = [
        pltpu.make_async_copy(src, dst, in_sem.at[i])
        for i, (src, dst) in enumerate(
            (
                (cot_ref, raw.at[3]),
                (q_ref, raw.at[0]),
                (k_ref, raw.at[1]),
                (v_ref, raw.at[2]),
                (w_hbm, w_ref),
                (count_hbm, count_ref),
                (bits_hbm, bits_ref),
            )
        )
    ]
    for copy in incoming:
        copy.start()

    barrier = pltpu.get_barrier_semaphore()

    def greet(to):
        pl.semaphore_signal(barrier, inc=1, device_id=to, device_id_type=MESH)

    def greet_plane(t, carry):
        xd, j, cd = lax.rem(x + t // 4 + 2, 4), lax.rem(t // 2, 2), lax.rem(t, 2)
        to = dev(xd, 2 * c + j, cd)

        @pl.when(jnp.logical_not((to[0] == dp) & (to[1] == seq)))
        def _():
            greet(to)

        @pl.when(cd == 0)
        def _():
            greet(dev(xd, 2 * (1 - c) + j, y // 2))

        return carry

    def planes_at(distance):
        return (
            (2 * lax.rem(z + distance, planes) + c, seq),
            (2 * lax.rem(z + planes - distance, planes) + c, seq),
        )

    if planes > 1:
        for to in planes_at(1):
            greet(to)
    lax.fori_loop(0, 16, greet_plane, 0)

    @pl.when(jnp.logical_not(own_side))
    def _():
        greet(dev(lax.rem(x + 1, 4), y, c))
        greet(dev(lax.rem(x + 3, 4), y, c))

    incoming[0].wait()
    cot_s[...] = jnp.swapaxes(raw[3], 0, 1)
    for i in range(3):
        incoming[1 + i].wait()
        qkv_s[i] = jnp.swapaxes(raw[i], 0, 1)

    greeted = 2 if planes > 1 else 0

    @pl.when(own_side)
    def _():
        pl.semaphore_wait(barrier, 23 + greeted)

    @pl.when(jnp.logical_not(own_side))
    def _():
        pl.semaphore_wait(barrier, 26 + greeted)

    def tell(step):
        if planes > 1:
            for to in planes_at(2**step):
                pl.semaphore_signal(known.at[step], inc=1, device_id=to, device_id_type=MESH)

    def learn(step):
        if planes > 1:
            pl.semaphore_wait(known.at[step], 2)
            if step < 2:
                tell(step + 1)

    tell(0)

    def push(src, dst, to, s_sem, r_sem):
        same = (to[0] == dp) & (to[1] == seq)

        @pl.when(same)
        def _():
            pltpu.make_async_copy(src, dst, r_sem).start()

        @pl.when(jnp.logical_not(same))
        def _():
            pltpu.make_async_remote_copy(
                src, dst, s_sem, r_sem, device_id=to, device_id_type=MESH
            ).start()

    def send(src, dst, to, s_sem, r_sem):
        pltpu.make_async_remote_copy(
            src, dst, s_sem, r_sem, device_id=to, device_id_type=MESH
        ).start()

    def landed(ref, sem):
        pltpu.make_async_copy(ref, ref, sem).wait()

    half = pl.ds(ROWS * (y % 2), ROWS)
    for j in range(2):
        to = dev(x, 2 * c + j, y // 2)
        push(cot_s.at[j], cot_all.at[2 * x + y // 2, half], to, ssem.at[0], rsem.at[12 + y % 2])

    def send_qkv(first, count, sem):
        def one(t, carry):
            xd, j, cd = lax.rem(x + t // 4 + 2, 4), lax.rem(t // 2, 2), lax.rem(t, 2)
            cols = pl.ds(pl.multiple_of(HEAD * (2 * xd + cd), HEAD), HEAD)
            push(
                qkv_s.at[pl.ds(first, count), j, :, cols],
                qkv_r.at[pl.ds(first, count), pl.ds(pl.multiple_of(ROWS * seq, ROWS), ROWS), :],
                dev(xd, 2 * c + j, cd),
                ssem.at[sem],
                rsem.at[sem],
            )
            return carry

        lax.fori_loop(0, 16, one, 0)

    send_qkv(0, 2, 2)
    send_qkv(2, 1, 9)

    incoming[5].wait()
    incoming[6].wait()

    @pl.when(own_side)
    def _():
        count = count_ref[y % 2]
        key_block = lax.broadcasted_iota(jnp.int32, (8, BLOCK), 0)
        lane = lax.broadcasted_iota(jnp.int32, (8, BLOCK), 1)
        for i in range(8):
            bits = bits_ref[y % 2, i]
            seen = (jnp.right_shift(jnp.full((8, BLOCK), bits, jnp.int32), key_block) & 1) == 1
            limit = jnp.where(seen, count - BLOCK * key_block, 0)
            aux[0:8, i * BLOCK : (i + 1) * BLOCK] = limit.astype(F32)
            live = lane + i * BLOCK < count
            aux[8:16, i * BLOCK : (i + 1) * BLOCK] = jnp.where(live, 1.0, 0.0)
        send(aux, aux, sibling, ssem.at[8], rsem.at[8])

    right = dev(lax.rem(x + 1, 4), y, c)
    left = dev(lax.rem(x + 3, 4), y, c)
    b_own = head
    b_left = 2 * lax.rem(x + 3, 4) + c
    b_right = 2 * lax.rem(x + 1, 4) + c
    b_far = 2 * lax.rem(x + 2, 4) + c
    low, high = pl.ds(0, ROWS), pl.ds(ROWS, ROWS)

    def ring_own(buf, s, r):
        for i, rows, to in (
            (0, low, right),
            (2, high, left),
            (1, high, right),
            (3, low, left),
            (6, low, sibling),
            (7, high, sibling),
        ):
            send(buf.at[b_own, rows], buf.at[b_own, rows], to, s.at[i], r.at[i])

    def ring_forward(buf, s, r):
        landed(buf.at[b_left, low], r.at[0])
        send(buf.at[b_left, low], buf.at[b_left, low], right, s.at[4], r.at[4])
        landed(buf.at[b_right, high], r.at[2])
        send(buf.at[b_right, high], buf.at[b_right, high], left, s.at[5], r.at[5])

    def ring_relay(buf, s, r):
        send(buf.at[b_left, low], buf.at[b_left, low], sibling, s.at[8], r.at[8])
        send(buf.at[b_right, high], buf.at[b_right, high], sibling, s.at[10], r.at[10])
        landed(buf.at[b_left, high], r.at[1])
        send(buf.at[b_left, high], buf.at[b_left, high], sibling, s.at[9], r.at[9])
        landed(buf.at[b_right, low], r.at[3])
        send(buf.at[b_right, low], buf.at[b_right, low], sibling, s.at[11], r.at[11])

    def ring_far(buf, s, r):
        landed(buf.at[b_far, low], r.at[4])
        send(buf.at[b_far, low], buf.at[b_far, low], sibling, s.at[12], r.at[12])
        landed(buf.at[b_far, high], r.at[5])
        send(buf.at[b_far, high], buf.at[b_far, high], sibling, s.at[13], r.at[13])

    def ring_rest(buf, r):
        other = 1 - 2 * c
        for i, b, rows in (
            (6, b_own, low),
            (7, b_own, high),
            (8, b_left, low),
            (9, b_left, high),
            (10, b_right, high),
            (11, b_right, low),
            (12, b_far, low),
            (13, b_far, high),
        ):
            landed(buf.at[b + other, rows], r.at[i])

    def ring_drain(buf, s):
        for i in range(14):
            landed(buf.at[0, low], s.at[i])

    landed(cot_all.at[b_own, low], rsem.at[12])
    landed(cot_all.at[b_own, high], rsem.at[13])
    ring_own(cot_all, cot_ssem, cot_sem)
    ring_forward(cot_all, cot_ssem, cot_sem)
    learn(0)

    @pl.when(jnp.logical_not(own_side))
    def _():
        landed(aux, rsem.at[8])

    landed(qkv_r.at[pl.ds(0, 2)], rsem.at[2])

    incoming[4].wait()
    for j in range(2):
        to = dev(x, 2 * c + j, y // 2)
        push(w_ref, w_all.at[2 * x + y // 2, half], to, ssem.at[1], rsem.at[14 + y % 2])

    factor = math.log2(math.e) / math.sqrt(HEAD)
    key_pos = lax.broadcasted_iota(jnp.int32, (BLOCK, IB), 0).astype(F32)

    def forward(i, carry):
        at = pl.multiple_of(i * IB, IB)
        here = pl.ds(at, IB)
        q_part = qkv_r[0, here, :]
        top = jnp.full((8, IB), MASKED, F32)
        for b in range(8):
            rows = pl.ds(b * BLOCK, BLOCK)
            s = lax.dot_general(qkv_r[1, rows, :], q_part, NT, preferred_element_type=F32)
            s = jnp.where(key_pos < aux[b : b + 1, here], s * factor, MASKED)
            scores[rows, :] = s
            top = jnp.maximum(top, jnp.max(s.reshape(BLOCK // 8, 8, IB), axis=0))
        top = jnp.max(top, axis=0, keepdims=True)
        total = jnp.zeros((8, IB), F32)
        for b in range(8):
            rows = pl.ds(b * BLOCK, BLOCK)
            e = jnp.exp2(scores[rows, :] - top)
            scores[rows, :] = e
            total = total + jnp.sum(e.reshape(BLOCK // 8, 8, IB), axis=0)
        inverse = 1.0 / jnp.sum(total, axis=0, keepdims=True)
        for b in range(8):
            rows = pl.ds(b * BLOCK, BLOCK)
            p = scores[rows, :] * inverse
            prob[i, rows, :] = p
            prob_b[rows, here] = p.astype(BF)
        return carry

    lax.fori_loop(0, 4, forward, 0)
    learn(1)
    ring_relay(cot_all, cot_ssem, cot_sem)
    kt[...] = qkv_r[1].astype(F32).T.astype(BF)
    landed(qkv_r.at[pl.ds(2, 1)], rsem.at[9])
    vt[...] = qkv_r[2].astype(F32).T.astype(BF)

    def mix(i, carry):
        here = pl.ds(pl.multiple_of(i * IB, IB), IB)
        mixed = jnp.dot(vt[...], prob_b[:, here], preferred_element_type=F32)
        mixed = jnp.where(aux[8:9, here] > 0.5, mixed, 0.0)
        att_t[:, here] = mixed.astype(BF)
        att_n[here, :] = mixed.T.astype(BF)
        return carry

    lax.fori_loop(0, 4, mix, 0)

    my_cols = pl.ds(pl.multiple_of(HEAD * head, HEAD), HEAD)

    def give_back(src, dst, s_sem, r_sem, first, count):
        def one(t, carry):
            to = first + t if count < 16 else lax.rem(seq + t, 16)
            push(
                src.at[pl.ds(pl.multiple_of(ROWS * to, ROWS), ROWS), :],
                dst.at[y % 2, :, my_cols],
                (2 * z + y // 2, to),
                s_sem,
                r_sem,
            )
            return carry

        lax.fori_loop(0, count, one, 0)

    ring_far(cot_all, cot_ssem, cot_sem)
    ring_rest(cot_all, cot_sem)

    cot_rows = cot_all[...].reshape(NODES, WIDTH)
    for h in range(2):
        for cd in range(2):
            edge = 512 * cd + 256 * h
            part[:, edge : edge + 256] = jnp.dot(
                att_t[...], cot_rows[:, edge : edge + 256], preferred_element_type=F32
            ).astype(BF)
            for r in range(2):
                push(
                    part.at[pl.ds(ROWS * r, ROWS), pl.ds(edge, 256)],
                    ry.at[h, y],
                    dev(x, 2 * c + r, cd),
                    ssem.at[7],
                    rsem.at[7 if h == 0 else 10],
                )
    landed(w_all.at[b_own, low], rsem.at[14])
    landed(w_all.at[b_own, high], rsem.at[15])
    ring_own(w_all, w_ssem, w_sem)
    for b in range(8):
        rows = pl.ds(b * BLOCK, BLOCK)
        g = lax.dot_general(cot_all[b], w_all[b_own], NT, preferred_element_type=F32)
        gt = jnp.where(aux[8:9, b * BLOCK : (b + 1) * BLOCK] > 0.5, g.T, 0.0)
        ag_t[:, rows] = gt.astype(BF)
        ag_n[rows, :] = gt.T.astype(BF)

    dqkv_n[2] = jnp.dot(prob_b[...], ag_n[...], preferred_element_type=F32).astype(BF)

    scale = 1.0 / math.sqrt(HEAD)

    def backward(step, carry):
        i = lax.rem(x + step, 4)
        at = pl.multiple_of(i * IB, IB)
        here = pl.ds(at, IB)
        g_part = ag_n[here, :]
        centre = jnp.sum(
            ag_t[:, here].astype(F32) * att_t[:, here].astype(F32), axis=0, keepdims=True
        )
        for b in range(8):
            rows = pl.ds(b * BLOCK, BLOCK)
            pg = lax.dot_general(qkv_r[2, rows, :], g_part, NT, preferred_element_type=F32)
            sgrad[rows, here] = (prob[i, rows, :] * ((pg - centre) * scale)).astype(BF)
        dq = jnp.dot(kt[...], sgrad[:, here], preferred_element_type=F32)
        dqkv_n[0, here, :] = dq.T.astype(BF)
        return carry

    def return_dq(step, carry):
        i = lax.rem(x + step, 4)
        give_back(dqkv_n.at[0], dqkv_ret.at[0], ssem.at[4], rsem.at[4], 4 * i, 4)
        return carry

    def corner(p, edge):
        q = p // 2
        return (
            pl.ds(pl.multiple_of(16 * lax.rem(q, 4), 16), 16),
            pl.ds(pl.multiple_of(edge + 128 * (q // 4), 128), 128),
        )

    def to_planes(h):
        landed(ry.at[h], rsem.at[7 if h == 0 else 10])
        total = ry[h, 0].astype(F32) + ry[h, 1].astype(F32)
        total = total + ry[h, 2].astype(F32) + ry[h, 3].astype(F32)
        zsrc[h] = total.astype(BF)
        if planes == 1:
            zag[:, pl.ds(pl.multiple_of(512 * c + 256 * h, 256), 256)] = (
                total * (1.0 / 256.0)
            ).astype(BF)
            return

        def send_z(t, carry):
            zd = 2 * lax.rem(z // 2 + t + 4, planes // 2) + h
            rows, cols = corner(zd, 0)
            push(zsrc.at[h, rows, cols], zr.at[z], (2 * zd + c, seq), ssem.at[10], rsem.at[16])
            return carry

        lax.fori_loop(0, planes // 2, send_z, 0)

    lax.fori_loop(0, 1, backward, 0)
    learn(2)
    to_planes(0)
    lax.fori_loop(1, 2, backward, 0)
    to_planes(1)
    give_back(dqkv_n.at[2], dqkv_ret.at[2], ssem.at[6], rsem.at[6], 0, 16)
    lax.fori_loop(0, 2, return_dq, 0)
    lax.fori_loop(2, 4, backward, 0)
    lax.fori_loop(2, 4, return_dq, 0)
    dqkv_n[1] = jnp.dot(sgrad[...], qkv_r[0], preferred_element_type=F32).astype(BF)
    give_back(dqkv_n.at[1], dqkv_ret.at[1], ssem.at[5], rsem.at[5], 0, 16)
    give_back(att_n, att_ret, ssem.at[3], rsem.at[3], 0, 16)
    ring_forward(w_all, w_ssem, w_sem)

    if planes > 1:
        landed(zr, rsem.at[16])
        zsum = zr[0].astype(F32)
        for p in range(1, planes):
            zsum = zsum + zr[p].astype(F32)
        zres[...] = (zsum * (1.0 / 256.0)).astype(BF)
        parity = lax.rem(z, 2)
        rows, cols = corner(z, 512 * c + 256 * parity)

        def spread(t, carry):
            zd = lax.rem(z + t + planes // 2, planes)
            to = (2 * zd + c, seq)
            push(zres, zag.at[rows, cols], to, ssem.at[11], rsem.at[17 + parity])
            return carry

        lax.fori_loop(0, planes, spread, 0)

    ring_relay(w_all, w_ssem, w_sem)
    ring_far(w_all, w_ssem, w_sem)
    landed(att_ret, rsem.at[3])
    ring_rest(w_all, w_sem)
    done = jnp.dot(
        att_ret[...].reshape(2 * ROWS, WIDTH),
        w_all[...].reshape(WIDTH, WIDTH),
        preferred_element_type=F32,
    ).astype(BF)
    outgoing = []

    def write(i, src, dst):
        outgoing.append(pltpu.make_async_copy(src, dst, out_sem.at[i]))
        outgoing[-1].start()

    mixed_rows[3] = jnp.swapaxes(done.reshape(2, ROWS, WIDTH), 0, 1)
    write(3, mixed_rows.at[3], out_ref)
    for i, ref in ((2, dv_ref), (0, dq_ref), (1, dk_ref)):
        landed(dqkv_ret.at[i], rsem.at[4 + i])
        mixed_rows[i] = jnp.swapaxes(dqkv_ret[i], 0, 1)
        write(i, mixed_rows.at[i], ref)

    for h in range(2):
        mine = zag.at[:, pl.ds(pl.multiple_of(512 * c + 256 * h, 256), 256)]
        if planes > 1:
            landed(mine, rsem.at[17 + h])
        send(mine, mine, sibling, ssem.at[12 + h], rsem.at[19 + h])
    for h in range(2):
        landed(zag.at[:, pl.ds(pl.multiple_of(512 - 512 * c + 256 * h, 256), 256)], rsem.at[19 + h])
    wg_f32[...] = zag[...].astype(F32)
    write(4, wg_f32, grad_ref)

    def left_here(sem, whole, short, is_short):
        @pl.when(is_short)
        def _():
            landed(short, sem)

        @pl.when(jnp.logical_not(is_short))
        def _():
            landed(whole, sem)

    @pl.when(own_side)
    def _():
        landed(aux, ssem.at[8])

    left_here(ssem.at[0], cot_s, cot_s.at[0], own_side)
    left_here(ssem.at[1], cot_s, cot_s.at[0], own_side)
    most = pl.ds(0, 15 * ROWS)
    left_here(ssem.at[2], qkv_r.at[0:2], qkv_r.at[0:2, most], own_side)
    left_here(ssem.at[9], qkv_r.at[2], qkv_r.at[2, most], own_side)
    left_here(ssem.at[3], att_n, att_n.at[most], own_side)
    for i in range(3):
        left_here(ssem.at[4 + i], dqkv_n.at[i], dqkv_n.at[i, most], own_side)
    left_here(ssem.at[7], ry, ry.at[:, pl.ds(0, 3)], own_side)
    if planes > 1:
        landed(zr.at[pl.ds(0, planes - 1)], ssem.at[10])
        landed(zr.at[pl.ds(0, planes - 1)], ssem.at[11])
    for h in range(2):
        landed(zag.at[:, pl.ds(256 * h, 256)], ssem.at[12 + h])
    ring_drain(cot_all, cot_ssem)
    ring_drain(w_all, w_ssem)
    for copy in outgoing:
        copy.wait()


def finish(*refs):
    held, sem = refs[10:15], refs[15]
    inward = [pltpu.make_async_copy(refs[i], held[i], sem.at[i]) for i in range(5)]
    outward = [pltpu.make_async_copy(held[i], refs[5 + i], sem.at[5 + i]) for i in range(5)]
    for copy in inward:
        copy.start()
    for first, second in zip(inward, outward):
        first.wait()
        second.start()
    for copy in outward:
        copy.wait()


def on_device(queries, key_rows, value_rows, cotangent, out_weight, node_counts, edge_bits):
    planes = lax.axis_size("dp") // 2
    hbm = pl.BlockSpec(memory_space=pltpu.HBM)
    most_vmem = 60 * 1024 * 1024
    rows3 = jax.ShapeDtypeStruct((ROWS, 2, WIDTH), BF)
    grad = jax.ShapeDtypeStruct((ROWS, WIDTH), F32)
    dma = pltpu.SemaphoreType.DMA
    shapes = (rows3, rows3, rows3, rows3, grad)
    results = pl.pallas_call(
        functools.partial(kernel, planes),
        out_shape=shapes,
        in_specs=[hbm] * 7,
        out_specs=(hbm,) * 5,
        scratch_shapes=[
            pltpu.VMEM((4, ROWS, 2, WIDTH), BF),
            pltpu.VMEM((ROWS, WIDTH), BF),
            pltpu.SMEM((2,), jnp.int32),
            pltpu.SMEM((2, 8), jnp.int32),
            pltpu.VMEM((3, 2, ROWS, WIDTH), BF),
            pltpu.VMEM((2, ROWS, WIDTH), BF),
            pltpu.VMEM((3, NODES, HEAD), BF),
            pltpu.VMEM((16, NODES), F32),
            pltpu.VMEM((8, BLOCK, WIDTH), BF),
            pltpu.VMEM((8, BLOCK, WIDTH), BF),
            pltpu.VMEM((NODES, IB), F32),
            pltpu.VMEM((NODES // IB, NODES, IB), F32),
            pltpu.VMEM((NODES, NODES), BF),
            pltpu.VMEM((NODES, NODES), BF),
            pltpu.VMEM((HEAD, NODES), BF),
            pltpu.VMEM((NODES, HEAD), BF),
            pltpu.VMEM((NODES, HEAD), BF),
            pltpu.VMEM((HEAD, NODES), BF),
            pltpu.VMEM((HEAD, NODES), BF),
            pltpu.VMEM((HEAD, NODES), BF),
            pltpu.VMEM((3, NODES, HEAD), BF),
            pltpu.VMEM((2, ROWS, WIDTH), BF),
            pltpu.VMEM((3, 2, ROWS, WIDTH), BF),
            pltpu.VMEM((HEAD, WIDTH), BF),
            pltpu.VMEM((2, 4, ROWS, 256), BF),
            pltpu.VMEM((2, ROWS, 256), BF),
            pltpu.VMEM((16, 16, 128), BF),
            pltpu.VMEM((16, 128), BF),
            pltpu.VMEM((ROWS, WIDTH), BF),
            pltpu.VMEM((4, ROWS, 2, WIDTH), BF),
            pltpu.VMEM((ROWS, WIDTH), F32),
            dma((7,)),
            dma((5,)),
            dma((14,)),
            dma((21,)),
            dma((14,)),
            dma((14,)),
            dma((14,)),
            dma((14,)),
            pltpu.SemaphoreType.REGULAR((3,)),
        ],
        compiler_params=pltpu.CompilerParams(
            collective_id=0, has_side_effects=True, vmem_limit_bytes=most_vmem
        ),
        cost_estimate=pl.CostEstimate(
            flops=3_000_000_000, bytes_accessed=3_000_000, transcendentals=1_000_000
        ),
        name="sublayer",
    )(
        queries,
        key_rows,
        value_rows,
        cotangent,
        out_weight,
        node_counts,
        edge_bits.reshape(2, 8),
    )
    return pl.pallas_call(
        finish,
        out_shape=shapes,
        in_specs=[hbm] * 5,
        out_specs=(hbm,) * 5,
        scratch_shapes=[pltpu.VMEM(one.shape, one.dtype) for one in shapes] + [dma((10,))],
        compiler_params=pltpu.CompilerParams(vmem_limit_bytes=most_vmem),
        name="results",
    )(*results)


def solution(mesh):
    rows = P("seq", "dp", None)
    weight = P("seq", None)
    return jax.shard_map(
        on_device,
        mesh=mesh,
        in_specs=(rows, rows, rows, rows, weight, P("dp"), P("dp", None, None)),
        out_specs=(rows, rows, rows, rows, weight),
        check_vma=False,
    )
```

```python
import functools
import math

import jax
import jax.numpy as jnp
from jax import lax
from jax.experimental import pallas as pl
from jax.experimental.pallas import tpu as pltpu
from jax.sharding import PartitionSpec as P

HEAD = 128
BLOCK = 128
NODES = 1024
WIDTH = 1024
ROWS = 64
IB = 256
MESH = pl.DeviceIdType.MESH
BF = jnp.bfloat16
F32 = jnp.float32
NT = (((1,), (1,)), ((), ()))
MASKED = -1e30


def kernel(
    planes,
    q_ref,
    k_ref,
    v_ref,
    cot_ref,
    w_hbm,
    count_hbm,
    bits_hbm,
    out_ref,
    dq_ref,
    dk_ref,
    dv_ref,
    grad_ref,
    raw,
    w_ref,
    count_ref,
    bits_ref,
    qkv_s,
    cot_s,
    qkv_r,
    aux,
    cot_all,
    w_all,
    scores,
    prob,
    prob_b,
    sgrad,
    att_t,
    att_n,
    ag_n,
    ag_t,
    vt,
    kt,
    dqkv_n,
    att_ret,
    dqkv_ret,
    part,
    ry,
    zsrc,
    zr,
    zres,
    zag,
    mixed_rows,
    wg_f32,
    in_sem,
    out_sem,
    ssem,
    rsem,
    cot_sem,
    w_sem,
    cot_ssem,
    w_ssem,
    known,
):
    dp = lax.axis_index("dp")
    seq = lax.axis_index("seq")
    z, c = dp // 2, dp % 2
    x, y = seq // 4, seq % 4
    head = 2 * x + c
    own_side = c == y // 2

    def dev(xd, yd, cd):
        return (2 * z + cd, 4 * xd + yd)

    sibling = dev(x, y, 1 - c)

    incoming = [
        pltpu.make_async_copy(src, dst, in_sem.at[i])
        for i, (src, dst) in enumerate(
            (
                (cot_ref, raw.at[3]),
                (q_ref, raw.at[0]),
                (k_ref, raw.at[1]),
                (v_ref, raw.at[2]),
                (w_hbm, w_ref),
                (count_hbm, count_ref),
                (bits_hbm, bits_ref),
            )
        )
    ]
    for copy in incoming:
        copy.start()

    barrier = pltpu.get_barrier_semaphore()

    def greet(to):
        pl.semaphore_signal(barrier, inc=1, device_id=to, device_id_type=MESH)

    def greet_plane(t, carry):
        xd, j, cd = lax.rem(x + t // 4 + 2, 4), lax.rem(t // 2, 2), lax.rem(t, 2)
        to = dev(xd, 2 * c + j, cd)

        @pl.when(jnp.logical_not((to[0] == dp) & (to[1] == seq)))
        def _():
            greet(to)

        @pl.when(cd == 0)
        def _():
            greet(dev(xd, 2 * (1 - c) + j, y // 2))

        return carry

    def planes_at(distance):
        return (
            (2 * lax.rem(z + distance, planes) + c, seq),
            (2 * lax.rem(z + planes - distance, planes) + c, seq),
        )

    if planes > 1:
        for to in planes_at(1):
            greet(to)
    lax.fori_loop(0, 16, greet_plane, 0)

    @pl.when(jnp.logical_not(own_side))
    def _():
        greet(dev(lax.rem(x + 1, 4), y, c))
        greet(dev(lax.rem(x + 3, 4), y, c))

    incoming[0].wait()
    cot_s[...] = jnp.swapaxes(raw[3], 0, 1)
    for i in range(3):
        incoming[1 + i].wait()
        qkv_s[i] = jnp.swapaxes(raw[i], 0, 1)

    greeted = 2 if planes > 1 else 0

    @pl.when(own_side)
    def _():
        pl.semaphore_wait(barrier, 23 + greeted)

    @pl.when(jnp.logical_not(own_side))
    def _():
        pl.semaphore_wait(barrier, 26 + greeted)

    def tell(step):
        if planes > 1:
            for to in planes_at(2**step):
                pl.semaphore_signal(known.at[step], inc=1, device_id=to, device_id_type=MESH)

    def learn(step):
        if planes > 1:
            pl.semaphore_wait(known.at[step], 2)
            if step < 2:
                tell(step + 1)

    tell(0)

    def push(src, dst, to, s_sem, r_sem):
        same = (to[0] == dp) & (to[1] == seq)

        @pl.when(same)
        def _():
            pltpu.make_async_copy(src, dst, r_sem).start()

        @pl.when(jnp.logical_not(same))
        def _():
            pltpu.make_async_remote_copy(
                src, dst, s_sem, r_sem, device_id=to, device_id_type=MESH
            ).start()

    def send(src, dst, to, s_sem, r_sem):
        pltpu.make_async_remote_copy(
            src, dst, s_sem, r_sem, device_id=to, device_id_type=MESH
        ).start()

    def landed(ref, sem):
        pltpu.make_async_copy(ref, ref, sem).wait()

    half = pl.ds(ROWS * (y % 2), ROWS)
    for j in range(2):
        to = dev(x, 2 * c + j, y // 2)
        push(cot_s.at[j], cot_all.at[2 * x + y // 2, half], to, ssem.at[0], rsem.at[12 + y % 2])

    def send_qkv(first, count, sem):
        def one(t, carry):
            xd, j, cd = lax.rem(x + t // 4 + 2, 4), lax.rem(t // 2, 2), lax.rem(t, 2)
            cols = pl.ds(pl.multiple_of(HEAD * (2 * xd + cd), HEAD), HEAD)
            push(
                qkv_s.at[pl.ds(first, count), j, :, cols],
                qkv_r.at[pl.ds(first, count), pl.ds(pl.multiple_of(ROWS * seq, ROWS), ROWS), :],
                dev(xd, 2 * c + j, cd),
                ssem.at[sem],
                rsem.at[sem],
            )
            return carry

        lax.fori_loop(0, 16, one, 0)

    send_qkv(0, 2, 2)
    send_qkv(2, 1, 9)

    incoming[5].wait()
    incoming[6].wait()

    @pl.when(own_side)
    def _():
        count = count_ref[y % 2]
        key_block = lax.broadcasted_iota(jnp.int32, (8, BLOCK), 0)
        lane = lax.broadcasted_iota(jnp.int32, (8, BLOCK), 1)
        for i in range(8):
            bits = bits_ref[y % 2, i]
            seen = (jnp.right_shift(jnp.full((8, BLOCK), bits, jnp.int32), key_block) & 1) == 1
            limit = jnp.where(seen, count - BLOCK * key_block, 0)
            aux[0:8, i * BLOCK : (i + 1) * BLOCK] = limit.astype(F32)
            live = lane + i * BLOCK < count
            aux[8:16, i * BLOCK : (i + 1) * BLOCK] = jnp.where(live, 1.0, 0.0)
        send(aux, aux, sibling, ssem.at[8], rsem.at[8])

    incoming[4].wait()
    for j in range(2):
        to = dev(x, 2 * c + j, y // 2)
        push(w_ref, w_all.at[2 * x + y // 2, half], to, ssem.at[1], rsem.at[14 + y % 2])

    right = dev(lax.rem(x + 1, 4), y, c)
    left = dev(lax.rem(x + 3, 4), y, c)
    b_own = head
    b_left = 2 * lax.rem(x + 3, 4) + c
    b_right = 2 * lax.rem(x + 1, 4) + c
    b_far = 2 * lax.rem(x + 2, 4) + c
    low, high = pl.ds(0, ROWS), pl.ds(ROWS, ROWS)

    def ring_own(buf, s, r):
        for i, rows, to in (
            (0, low, right),
            (2, high, left),
            (1, high, right),
            (3, low, left),
            (6, low, sibling),
            (7, high, sibling),
        ):
            send(buf.at[b_own, rows], buf.at[b_own, rows], to, s.at[i], r.at[i])

    def ring_forward(buf, s, r):
        landed(buf.at[b_left, low], r.at[0])
        send(buf.at[b_left, low], buf.at[b_left, low], right, s.at[4], r.at[4])
        landed(buf.at[b_right, high], r.at[2])
        send(buf.at[b_right, high], buf.at[b_right, high], left, s.at[5], r.at[5])

    def ring_relay(buf, s, r):
        send(buf.at[b_left, low], buf.at[b_left, low], sibling, s.at[8], r.at[8])
        send(buf.at[b_right, high], buf.at[b_right, high], sibling, s.at[10], r.at[10])
        landed(buf.at[b_left, high], r.at[1])
        send(buf.at[b_left, high], buf.at[b_left, high], sibling, s.at[9], r.at[9])
        landed(buf.at[b_right, low], r.at[3])
        send(buf.at[b_right, low], buf.at[b_right, low], sibling, s.at[11], r.at[11])

    def ring_far(buf, s, r):
        landed(buf.at[b_far, low], r.at[4])
        send(buf.at[b_far, low], buf.at[b_far, low], sibling, s.at[12], r.at[12])
        landed(buf.at[b_far, high], r.at[5])
        send(buf.at[b_far, high], buf.at[b_far, high], sibling, s.at[13], r.at[13])

    def ring_rest(buf, r):
        other = 1 - 2 * c
        for i, b, rows in (
            (6, b_own, low),
            (7, b_own, high),
            (8, b_left, low),
            (9, b_left, high),
            (10, b_right, high),
            (11, b_right, low),
            (12, b_far, low),
            (13, b_far, high),
        ):
            landed(buf.at[b + other, rows], r.at[i])

    def ring_drain(buf, s):
        for i in range(14):
            landed(buf.at[0, low], s.at[i])

    landed(cot_all.at[b_own, low], rsem.at[12])
    landed(cot_all.at[b_own, high], rsem.at[13])
    ring_own(cot_all, cot_ssem, cot_sem)
    ring_forward(cot_all, cot_ssem, cot_sem)
    learn(0)

    @pl.when(jnp.logical_not(own_side))
    def _():
        landed(aux, rsem.at[8])

    landed(qkv_r.at[pl.ds(0, 2)], rsem.at[2])

    factor = math.log2(math.e) / math.sqrt(HEAD)
    key_pos = lax.broadcasted_iota(jnp.int32, (BLOCK, IB), 0).astype(F32)

    def forward(i, carry):
        at = pl.multiple_of(i * IB, IB)
        here = pl.ds(at, IB)
        q_part = qkv_r[0, here, :]
        top = jnp.full((8, IB), MASKED, F32)
        for b in range(8):
            rows = pl.ds(b * BLOCK, BLOCK)
            s = lax.dot_general(qkv_r[1, rows, :], q_part, NT, preferred_element_type=F32)
            s = jnp.where(key_pos < aux[b : b + 1, here], s * factor, MASKED)
            scores[rows, :] = s
            top = jnp.maximum(top, jnp.max(s.reshape(BLOCK // 8, 8, IB), axis=0))
        top = jnp.max(top, axis=0, keepdims=True)
        total = jnp.zeros((8, IB), F32)
        for b in range(8):
            rows = pl.ds(b * BLOCK, BLOCK)
            e = jnp.exp2(scores[rows, :] - top)
            scores[rows, :] = e
            total = total + jnp.sum(e.reshape(BLOCK // 8, 8, IB), axis=0)
        inverse = 1.0 / jnp.sum(total, axis=0, keepdims=True)
        for b in range(8):
            rows = pl.ds(b * BLOCK, BLOCK)
            p = scores[rows, :] * inverse
            prob[i, rows, :] = p
            prob_b[rows, here] = p.astype(BF)
        return carry

    lax.fori_loop(0, 4, forward, 0)
    learn(1)
    ring_relay(cot_all, cot_ssem, cot_sem)
    landed(w_all.at[b_own, low], rsem.at[14])
    landed(w_all.at[b_own, high], rsem.at[15])
    ring_own(w_all, w_ssem, w_sem)
    kt[...] = qkv_r[1].astype(F32).T.astype(BF)
    landed(qkv_r.at[pl.ds(2, 1)], rsem.at[9])
    vt[...] = qkv_r[2].astype(F32).T.astype(BF)

    def mix(i, carry):
        here = pl.ds(pl.multiple_of(i * IB, IB), IB)
        mixed = jnp.dot(vt[...], prob_b[:, here], preferred_element_type=F32)
        mixed = jnp.where(aux[8:9, here] > 0.5, mixed, 0.0)
        att_t[:, here] = mixed.astype(BF)
        att_n[here, :] = mixed.T.astype(BF)
        return carry

    lax.fori_loop(0, 4, mix, 0)

    my_cols = pl.ds(pl.multiple_of(HEAD * head, HEAD), HEAD)

    def give_back(src, dst, s_sem, r_sem, first, count):
        def one(t, carry):
            to = first + t if count < 16 else lax.rem(seq + t, 16)
            push(
                src.at[pl.ds(pl.multiple_of(ROWS * to, ROWS), ROWS), :],
                dst.at[y % 2, :, my_cols],
                (2 * z + y // 2, to),
                s_sem,
                r_sem,
            )
            return carry

        lax.fori_loop(0, count, one, 0)

    ring_far(cot_all, cot_ssem, cot_sem)
    ring_rest(cot_all, cot_sem)

    cot_rows = cot_all[...].reshape(NODES, WIDTH)
    for h in range(2):
        for cd in range(2):
            edge = 512 * cd + 256 * h
            part[:, edge : edge + 256] = jnp.dot(
                att_t[...], cot_rows[:, edge : edge + 256], preferred_element_type=F32
            ).astype(BF)
            for r in range(2):
                push(
                    part.at[pl.ds(ROWS * r, ROWS), pl.ds(edge, 256)],
                    ry.at[h, y],
                    dev(x, 2 * c + r, cd),
                    ssem.at[7],
                    rsem.at[7 if h == 0 else 10],
                )
    for b in range(8):
        rows = pl.ds(b * BLOCK, BLOCK)
        g = lax.dot_general(cot_all[b], w_all[b_own], NT, preferred_element_type=F32)
        gt = jnp.where(aux[8:9, b * BLOCK : (b + 1) * BLOCK] > 0.5, g.T, 0.0)
        ag_t[:, rows] = gt.astype(BF)
        ag_n[rows, :] = gt.T.astype(BF)

    give_back(att_n, att_ret, ssem.at[3], rsem.at[3], 0, 16)
    dqkv_n[2] = jnp.dot(prob_b[...], ag_n[...], preferred_element_type=F32).astype(BF)

    scale = 1.0 / math.sqrt(HEAD)

    def backward(step, carry):
        i = lax.rem(x + step, 4)
        at = pl.multiple_of(i * IB, IB)
        here = pl.ds(at, IB)
        g_part = ag_n[here, :]
        centre = jnp.sum(
            ag_t[:, here].astype(F32) * att_t[:, here].astype(F32), axis=0, keepdims=True
        )
        for b in range(8):
            rows = pl.ds(b * BLOCK, BLOCK)
            pg = lax.dot_general(qkv_r[2, rows, :], g_part, NT, preferred_element_type=F32)
            sgrad[rows, here] = (prob[i, rows, :] * ((pg - centre) * scale)).astype(BF)
        dq = jnp.dot(kt[...], sgrad[:, here], preferred_element_type=F32)
        dqkv_n[0, here, :] = dq.T.astype(BF)
        return carry

    def return_dq(step, carry):
        i = lax.rem(x + step, 4)
        give_back(dqkv_n.at[0], dqkv_ret.at[0], ssem.at[4], rsem.at[4], 4 * i, 4)
        return carry

    def corner(p, edge):
        q = p // 2
        return (
            pl.ds(pl.multiple_of(16 * lax.rem(q, 4), 16), 16),
            pl.ds(pl.multiple_of(edge + 128 * (q // 4), 128), 128),
        )

    def to_planes(h):
        landed(ry.at[h], rsem.at[7 if h == 0 else 10])
        total = ry[h, 0].astype(F32) + ry[h, 1].astype(F32)
        total = total + ry[h, 2].astype(F32) + ry[h, 3].astype(F32)
        zsrc[h] = total.astype(BF)
        if planes == 1:
            zag[:, pl.ds(pl.multiple_of(512 * c + 256 * h, 256), 256)] = (
                total * (1.0 / 256.0)
            ).astype(BF)
            return

        def send_z(t, carry):
            zd = 2 * lax.rem(z // 2 + t + 4, planes // 2) + h
            rows, cols = corner(zd, 0)
            push(zsrc.at[h, rows, cols], zr.at[z], (2 * zd + c, seq), ssem.at[10], rsem.at[16])
            return carry

        lax.fori_loop(0, planes // 2, send_z, 0)

    lax.fori_loop(0, 1, backward, 0)
    learn(2)
    to_planes(0)
    give_back(dqkv_n.at[2], dqkv_ret.at[2], ssem.at[6], rsem.at[6], 0, 16)
    ring_forward(w_all, w_ssem, w_sem)
    lax.fori_loop(1, 2, backward, 0)
    to_planes(1)
    ring_relay(w_all, w_ssem, w_sem)
    lax.fori_loop(0, 2, return_dq, 0)
    lax.fori_loop(2, 4, backward, 0)
    lax.fori_loop(2, 4, return_dq, 0)
    dqkv_n[1] = jnp.dot(sgrad[...], qkv_r[0], preferred_element_type=F32).astype(BF)
    give_back(dqkv_n.at[1], dqkv_ret.at[1], ssem.at[5], rsem.at[5], 0, 16)

    if planes > 1:
        landed(zr, rsem.at[16])
        zsum = zr[0].astype(F32)
        for p in range(1, planes):
            zsum = zsum + zr[p].astype(F32)
        zres[...] = (zsum * (1.0 / 256.0)).astype(BF)
        parity = lax.rem(z, 2)
        rows, cols = corner(z, 512 * c + 256 * parity)

        def spread(t, carry):
            zd = lax.rem(z + t + planes // 2, planes)
            to = (2 * zd + c, seq)
            push(zres, zag.at[rows, cols], to, ssem.at[11], rsem.at[17 + parity])
            return carry

        lax.fori_loop(0, planes, spread, 0)

    ring_far(w_all, w_ssem, w_sem)
    landed(att_ret, rsem.at[3])
    ring_rest(w_all, w_sem)
    done = jnp.dot(
        att_ret[...].reshape(2 * ROWS, WIDTH),
        w_all[...].reshape(WIDTH, WIDTH),
        preferred_element_type=F32,
    ).astype(BF)
    outgoing = []

    def write(i, src, dst):
        outgoing.append(pltpu.make_async_copy(src, dst, out_sem.at[i]))
        outgoing[-1].start()

    mixed_rows[3] = jnp.swapaxes(done.reshape(2, ROWS, WIDTH), 0, 1)
    write(3, mixed_rows.at[3], out_ref)
    for i, ref in ((2, dv_ref), (0, dq_ref), (1, dk_ref)):
        landed(dqkv_ret.at[i], rsem.at[4 + i])
        mixed_rows[i] = jnp.swapaxes(dqkv_ret[i], 0, 1)
        write(i, mixed_rows.at[i], ref)

    for h in range(2):
        mine = zag.at[:, pl.ds(pl.multiple_of(512 * c + 256 * h, 256), 256)]
        if planes > 1:
            landed(mine, rsem.at[17 + h])
        send(mine, mine, sibling, ssem.at[12 + h], rsem.at[19 + h])
    for h in range(2):
        landed(zag.at[:, pl.ds(pl.multiple_of(512 - 512 * c + 256 * h, 256), 256)], rsem.at[19 + h])
    wg_f32[...] = zag[...].astype(F32)
    write(4, wg_f32, grad_ref)

    def left_here(sem, whole, short, is_short):
        @pl.when(is_short)
        def _():
            landed(short, sem)

        @pl.when(jnp.logical_not(is_short))
        def _():
            landed(whole, sem)

    @pl.when(own_side)
    def _():
        landed(aux, ssem.at[8])

    left_here(ssem.at[0], cot_s, cot_s.at[0], own_side)
    left_here(ssem.at[1], cot_s, cot_s.at[0], own_side)
    most = pl.ds(0, 15 * ROWS)
    left_here(ssem.at[2], qkv_r.at[0:2], qkv_r.at[0:2, most], own_side)
    left_here(ssem.at[9], qkv_r.at[2], qkv_r.at[2, most], own_side)
    left_here(ssem.at[3], att_n, att_n.at[most], own_side)
    for i in range(3):
        left_here(ssem.at[4 + i], dqkv_n.at[i], dqkv_n.at[i, most], own_side)
    left_here(ssem.at[7], ry, ry.at[:, pl.ds(0, 3)], own_side)
    if planes > 1:
        landed(zr.at[pl.ds(0, planes - 1)], ssem.at[10])
        landed(zr.at[pl.ds(0, planes - 1)], ssem.at[11])
    for h in range(2):
        landed(zag.at[:, pl.ds(256 * h, 256)], ssem.at[12 + h])
    ring_drain(cot_all, cot_ssem)
    ring_drain(w_all, w_ssem)
    for copy in outgoing:
        copy.wait()


def finish(*refs):
    held, sem = refs[10:15], refs[15]
    inward = [pltpu.make_async_copy(refs[i], held[i], sem.at[i]) for i in range(5)]
    outward = [pltpu.make_async_copy(held[i], refs[5 + i], sem.at[5 + i]) for i in range(5)]
    for copy in inward:
        copy.start()
    for first, second in zip(inward, outward):
        first.wait()
        second.start()
    for copy in outward:
        copy.wait()


def on_device(queries, key_rows, value_rows, cotangent, out_weight, node_counts, edge_bits):
    planes = lax.axis_size("dp") // 2
    hbm = pl.BlockSpec(memory_space=pltpu.HBM)
    most_vmem = 60 * 1024 * 1024
    rows3 = jax.ShapeDtypeStruct((ROWS, 2, WIDTH), BF)
    grad = jax.ShapeDtypeStruct((ROWS, WIDTH), F32)
    dma = pltpu.SemaphoreType.DMA
    shapes = (rows3, rows3, rows3, rows3, grad)
    results = pl.pallas_call(
        functools.partial(kernel, planes),
        out_shape=shapes,
        in_specs=[hbm] * 7,
        out_specs=(hbm,) * 5,
        scratch_shapes=[
            pltpu.VMEM((4, ROWS, 2, WIDTH), BF),
            pltpu.VMEM((ROWS, WIDTH), BF),
            pltpu.SMEM((2,), jnp.int32),
            pltpu.SMEM((2, 8), jnp.int32),
            pltpu.VMEM((3, 2, ROWS, WIDTH), BF),
            pltpu.VMEM((2, ROWS, WIDTH), BF),
            pltpu.VMEM((3, NODES, HEAD), BF),
            pltpu.VMEM((16, NODES), F32),
            pltpu.VMEM((8, BLOCK, WIDTH), BF),
            pltpu.VMEM((8, BLOCK, WIDTH), BF),
            pltpu.VMEM((NODES, IB), F32),
            pltpu.VMEM((NODES // IB, NODES, IB), F32),
            pltpu.VMEM((NODES, NODES), BF),
            pltpu.VMEM((NODES, NODES), BF),
            pltpu.VMEM((HEAD, NODES), BF),
            pltpu.VMEM((NODES, HEAD), BF),
            pltpu.VMEM((NODES, HEAD), BF),
            pltpu.VMEM((HEAD, NODES), BF),
            pltpu.VMEM((HEAD, NODES), BF),
            pltpu.VMEM((HEAD, NODES), BF),
            pltpu.VMEM((3, NODES, HEAD), BF),
            pltpu.VMEM((2, ROWS, WIDTH), BF),
            pltpu.VMEM((3, 2, ROWS, WIDTH), BF),
            pltpu.VMEM((HEAD, WIDTH), BF),
            pltpu.VMEM((2, 4, ROWS, 256), BF),
            pltpu.VMEM((2, ROWS, 256), BF),
            pltpu.VMEM((16, 16, 128), BF),
            pltpu.VMEM((16, 128), BF),
            pltpu.VMEM((ROWS, WIDTH), BF),
            pltpu.VMEM((4, ROWS, 2, WIDTH), BF),
            pltpu.VMEM((ROWS, WIDTH), F32),
            dma((7,)),
            dma((5,)),
            dma((14,)),
            dma((21,)),
            dma((14,)),
            dma((14,)),
            dma((14,)),
            dma((14,)),
            pltpu.SemaphoreType.REGULAR((3,)),
        ],
        compiler_params=pltpu.CompilerParams(
            collective_id=0, has_side_effects=True, vmem_limit_bytes=most_vmem
        ),
        cost_estimate=pl.CostEstimate(
            flops=3_000_000_000, bytes_accessed=3_000_000, transcendentals=1_000_000
        ),
        name="sublayer",
    )(
        queries,
        key_rows,
        value_rows,
        cotangent,
        out_weight,
        node_counts,
        edge_bits.reshape(2, 8),
    )
    return pl.pallas_call(
        finish,
        out_shape=shapes,
        in_specs=[hbm] * 5,
        out_specs=(hbm,) * 5,
        scratch_shapes=[pltpu.VMEM(one.shape, one.dtype) for one in shapes] + [dma((10,))],
        compiler_params=pltpu.CompilerParams(vmem_limit_bytes=most_vmem),
        name="results",
    )(*results)


def solution(mesh):
    rows = P("seq", "dp", None)
    weight = P("seq", None)
    return jax.shard_map(
        on_device,
        mesh=mesh,
        in_specs=(rows, rows, rows, rows, weight, P("dp"), P("dp", None, None)),
        out_specs=(rows, rows, rows, rows, weight),
        check_vma=False,
    )
```

```python
import functools
import math

import jax
import jax.numpy as jnp
from jax import lax
from jax.experimental import pallas as pl
from jax.experimental.pallas import tpu as pltpu
from jax.sharding import PartitionSpec as P

HEAD = 128
BLOCK = 128
NODES = 1024
WIDTH = 1024
ROWS = 64
IB = 256
MESH = pl.DeviceIdType.MESH
BF = jnp.bfloat16
F32 = jnp.float32
NT = (((1,), (1,)), ((), ()))
MASKED = -1e30


def kernel(
    planes,
    q_ref,
    k_ref,
    v_ref,
    cot_ref,
    w_hbm,
    count_hbm,
    bits_hbm,
    out_ref,
    dq_ref,
    dk_ref,
    dv_ref,
    grad_ref,
    raw,
    w_ref,
    count_ref,
    bits_ref,
    qkv_s,
    cot_s,
    qkv_r,
    aux,
    cot_all,
    w_all,
    scores,
    prob,
    prob_b,
    sgrad,
    att_t,
    att_n,
    ag_n,
    ag_t,
    vt,
    kt,
    dqkv_n,
    att_ret,
    dqkv_ret,
    part,
    ry,
    zsrc,
    zr,
    zres,
    zag,
    in_sem,
    ssem,
    rsem,
    cot_sem,
    w_sem,
    cot_ssem,
    w_ssem,
    known,
):
    dp = lax.axis_index("dp")
    seq = lax.axis_index("seq")
    z, c = dp // 2, dp % 2
    x, y = seq // 4, seq % 4
    head = 2 * x + c
    own_side = c == y // 2

    def dev(xd, yd, cd):
        return (2 * z + cd, 4 * xd + yd)

    sibling = dev(x, y, 1 - c)

    incoming = [
        pltpu.make_async_copy(src, dst, in_sem.at[i])
        for i, (src, dst) in enumerate(
            (
                (cot_ref, raw.at[3]),
                (q_ref, raw.at[0]),
                (k_ref, raw.at[1]),
                (v_ref, raw.at[2]),
                (w_hbm, w_ref),
                (count_hbm, count_ref),
                (bits_hbm, bits_ref),
            )
        )
    ]
    for copy in incoming:
        copy.start()

    barrier = pltpu.get_barrier_semaphore()

    def greet(to):
        pl.semaphore_signal(barrier, inc=1, device_id=to, device_id_type=MESH)

    def greet_plane(t, carry):
        xd, j, cd = lax.rem(x + t // 4 + 2, 4), lax.rem(t // 2, 2), lax.rem(t, 2)
        to = dev(xd, 2 * c + j, cd)

        @pl.when(jnp.logical_not((to[0] == dp) & (to[1] == seq)))
        def _():
            greet(to)

        @pl.when(cd == 0)
        def _():
            greet(dev(xd, 2 * (1 - c) + j, y // 2))

        return carry

    def planes_at(distance):
        return (
            (2 * lax.rem(z + distance, planes) + c, seq),
            (2 * lax.rem(z + planes - distance, planes) + c, seq),
        )

    if planes > 1:
        for to in planes_at(1):
            greet(to)
    lax.fori_loop(0, 16, greet_plane, 0)

    @pl.when(jnp.logical_not(own_side))
    def _():
        greet(dev(lax.rem(x + 1, 4), y, c))
        greet(dev(lax.rem(x + 3, 4), y, c))

    incoming[0].wait()
    cot_s[...] = jnp.swapaxes(raw[3], 0, 1)
    for i in range(3):
        incoming[1 + i].wait()
        qkv_s[i] = jnp.swapaxes(raw[i], 0, 1)

    greeted = 2 if planes > 1 else 0

    @pl.when(own_side)
    def _():
        pl.semaphore_wait(barrier, 23 + greeted)

    @pl.when(jnp.logical_not(own_side))
    def _():
        pl.semaphore_wait(barrier, 26 + greeted)

    def tell(step):
        if planes > 1:
            for to in planes_at(2**step):
                pl.semaphore_signal(known.at[step], inc=1, device_id=to, device_id_type=MESH)

    def learn(step):
        if planes > 1:
            pl.semaphore_wait(known.at[step], 2)
            if step < 2:
                tell(step + 1)

    tell(0)

    def push(src, dst, to, s_sem, r_sem):
        same = (to[0] == dp) & (to[1] == seq)

        @pl.when(same)
        def _():
            pltpu.make_async_copy(src, dst, r_sem).start()

        @pl.when(jnp.logical_not(same))
        def _():
            pltpu.make_async_remote_copy(
                src, dst, s_sem, r_sem, device_id=to, device_id_type=MESH
            ).start()

    def send(src, dst, to, s_sem, r_sem):
        pltpu.make_async_remote_copy(
            src, dst, s_sem, r_sem, device_id=to, device_id_type=MESH
        ).start()

    def landed(ref, sem):
        pltpu.make_async_copy(ref, ref, sem).wait()

    half = pl.ds(ROWS * (y % 2), ROWS)
    for j in range(2):
        to = dev(x, 2 * c + j, y // 2)
        push(cot_s.at[j], cot_all.at[2 * x + y // 2, half], to, ssem.at[0], rsem.at[12 + y % 2])

    def send_qkv(first, count, sem):
        def one(t, carry):
            xd, j, cd = lax.rem(x + t // 4 + 2, 4), lax.rem(t // 2, 2), lax.rem(t, 2)
            cols = pl.ds(pl.multiple_of(HEAD * (2 * xd + cd), HEAD), HEAD)
            push(
                qkv_s.at[pl.ds(first, count), j, :, cols],
                qkv_r.at[pl.ds(first, count), pl.ds(pl.multiple_of(ROWS * seq, ROWS), ROWS), :],
                dev(xd, 2 * c + j, cd),
                ssem.at[sem],
                rsem.at[sem],
            )
            return carry

        lax.fori_loop(0, 16, one, 0)

    send_qkv(0, 2, 2)
    send_qkv(2, 1, 9)

    incoming[5].wait()
    incoming[6].wait()

    @pl.when(own_side)
    def _():
        count = count_ref[y % 2]
        key_block = lax.broadcasted_iota(jnp.int32, (8, BLOCK), 0)
        lane = lax.broadcasted_iota(jnp.int32, (8, BLOCK), 1)
        for i in range(8):
            bits = bits_ref[y % 2, i]
            seen = (jnp.right_shift(jnp.full((8, BLOCK), bits, jnp.int32), key_block) & 1) == 1
            limit = jnp.where(seen, count - BLOCK * key_block, 0)
            aux[0:8, i * BLOCK : (i + 1) * BLOCK] = limit.astype(F32)
            live = lane + i * BLOCK < count
            aux[8:16, i * BLOCK : (i + 1) * BLOCK] = jnp.where(live, 1.0, 0.0)
        send(aux, aux, sibling, ssem.at[8], rsem.at[8])

    incoming[4].wait()
    for j in range(2):
        to = dev(x, 2 * c + j, y // 2)
        push(w_ref, w_all.at[2 * x + y // 2, half], to, ssem.at[1], rsem.at[14 + y % 2])

    right = dev(lax.rem(x + 1, 4), y, c)
    left = dev(lax.rem(x + 3, 4), y, c)
    b_own = head
    b_left = 2 * lax.rem(x + 3, 4) + c
    b_right = 2 * lax.rem(x + 1, 4) + c
    b_far = 2 * lax.rem(x + 2, 4) + c
    low, high = pl.ds(0, ROWS), pl.ds(ROWS, ROWS)

    def ring_own(buf, s, r):
        for i, rows, to in (
            (0, low, right),
            (2, high, left),
            (1, high, right),
            (3, low, left),
            (6, low, sibling),
            (7, high, sibling),
        ):
            send(buf.at[b_own, rows], buf.at[b_own, rows], to, s.at[i], r.at[i])

    def ring_forward(buf, s, r):
        landed(buf.at[b_left, low], r.at[0])
        send(buf.at[b_left, low], buf.at[b_left, low], right, s.at[4], r.at[4])
        landed(buf.at[b_right, high], r.at[2])
        send(buf.at[b_right, high], buf.at[b_right, high], left, s.at[5], r.at[5])

    def ring_relay(buf, s, r):
        send(buf.at[b_left, low], buf.at[b_left, low], sibling, s.at[8], r.at[8])
        send(buf.at[b_right, high], buf.at[b_right, high], sibling, s.at[10], r.at[10])
        landed(buf.at[b_left, high], r.at[1])
        send(buf.at[b_left, high], buf.at[b_left, high], sibling, s.at[9], r.at[9])
        landed(buf.at[b_right, low], r.at[3])
        send(buf.at[b_right, low], buf.at[b_right, low], sibling, s.at[11], r.at[11])

    def ring_far(buf, s, r):
        landed(buf.at[b_far, low], r.at[4])
        send(buf.at[b_far, low], buf.at[b_far, low], sibling, s.at[12], r.at[12])
        landed(buf.at[b_far, high], r.at[5])
        send(buf.at[b_far, high], buf.at[b_far, high], sibling, s.at[13], r.at[13])

    def ring_rest(buf, r):
        other = 1 - 2 * c
        for i, b, rows in (
            (6, b_own, low),
            (7, b_own, high),
            (8, b_left, low),
            (9, b_left, high),
            (10, b_right, high),
            (11, b_right, low),
            (12, b_far, low),
            (13, b_far, high),
        ):
            landed(buf.at[b + other, rows], r.at[i])

    def ring_drain(buf, s):
        for i in range(14):
            landed(buf.at[0, low], s.at[i])

    landed(cot_all.at[b_own, low], rsem.at[12])
    landed(cot_all.at[b_own, high], rsem.at[13])
    ring_own(cot_all, cot_ssem, cot_sem)
    ring_forward(cot_all, cot_ssem, cot_sem)
    learn(0)

    @pl.when(jnp.logical_not(own_side))
    def _():
        landed(aux, rsem.at[8])

    landed(qkv_r.at[pl.ds(0, 2)], rsem.at[2])

    factor = math.log2(math.e) / math.sqrt(HEAD)
    key_pos = lax.broadcasted_iota(jnp.int32, (BLOCK, IB), 0).astype(F32)

    def forward(i, carry):
        at = pl.multiple_of(i * IB, IB)
        here = pl.ds(at, IB)
        q_part = qkv_r[0, here, :]
        top = jnp.full((8, IB), MASKED, F32)
        for b in range(8):
            rows = pl.ds(b * BLOCK, BLOCK)
            s = lax.dot_general(qkv_r[1, rows, :], q_part, NT, preferred_element_type=F32)
            s = jnp.where(key_pos < aux[b : b + 1, here], s * factor, MASKED)
            scores[rows, :] = s
            top = jnp.maximum(top, jnp.max(s.reshape(BLOCK // 8, 8, IB), axis=0))
        top = jnp.max(top, axis=0, keepdims=True)
        total = jnp.zeros((8, IB), F32)
        for b in range(8):
            rows = pl.ds(b * BLOCK, BLOCK)
            e = jnp.exp2(scores[rows, :] - top)
            scores[rows, :] = e
            total = total + jnp.sum(e.reshape(BLOCK // 8, 8, IB), axis=0)
        inverse = 1.0 / jnp.sum(total, axis=0, keepdims=True)
        for b in range(8):
            rows = pl.ds(b * BLOCK, BLOCK)
            p = scores[rows, :] * inverse
            prob[i, rows, :] = p
            prob_b[rows, here] = p.astype(BF)
        return carry

    lax.fori_loop(0, 4, forward, 0)
    learn(1)
    ring_relay(cot_all, cot_ssem, cot_sem)
    landed(w_all.at[b_own, low], rsem.at[14])
    landed(w_all.at[b_own, high], rsem.at[15])
    ring_own(w_all, w_ssem, w_sem)
    kt[...] = qkv_r[1].astype(F32).T.astype(BF)
    landed(qkv_r.at[pl.ds(2, 1)], rsem.at[9])
    vt[...] = qkv_r[2].astype(F32).T.astype(BF)

    def mix(i, carry):
        here = pl.ds(pl.multiple_of(i * IB, IB), IB)
        mixed = jnp.dot(vt[...], prob_b[:, here], preferred_element_type=F32)
        mixed = jnp.where(aux[8:9, here] > 0.5, mixed, 0.0)
        att_t[:, here] = mixed.astype(BF)
        att_n[here, :] = mixed.T.astype(BF)
        return carry

    lax.fori_loop(0, 4, mix, 0)

    my_cols = pl.ds(pl.multiple_of(HEAD * head, HEAD), HEAD)

    def give_back(src, dst, s_sem, r_sem, first, count):
        def one(t, carry):
            to = first + lax.rem(t + y + 2, 4) if count < 16 else lax.rem(seq + t + 8, 16)
            push(
                src.at[pl.ds(pl.multiple_of(ROWS * to, ROWS), ROWS), :],
                dst.at[y % 2, :, my_cols],
                (2 * z + y // 2, to),
                s_sem,
                r_sem,
            )
            return carry

        lax.fori_loop(0, count, one, 0)

    ring_far(cot_all, cot_ssem, cot_sem)
    ring_rest(cot_all, cot_sem)

    cot_rows = cot_all[...].reshape(NODES, WIDTH)
    for h in range(2):
        for cd in range(2):
            edge = 512 * cd + 256 * h
            part[:, edge : edge + 256] = jnp.dot(
                att_t[...], cot_rows[:, edge : edge + 256], preferred_element_type=F32
            ).astype(BF)
            for r in range(2):
                push(
                    part.at[pl.ds(ROWS * r, ROWS), pl.ds(edge, 256)],
                    ry.at[h, y],
                    dev(x, 2 * c + r, cd),
                    ssem.at[7],
                    rsem.at[7 if h == 0 else 10],
                )
    for b in range(8):
        rows = pl.ds(b * BLOCK, BLOCK)
        g = lax.dot_general(cot_all[b], w_all[b_own], NT, preferred_element_type=F32)
        gt = jnp.where(aux[8:9, b * BLOCK : (b + 1) * BLOCK] > 0.5, g.T, 0.0)
        ag_t[:, rows] = gt.astype(BF)
        ag_n[rows, :] = gt.T.astype(BF)

    give_back(att_n, att_ret, ssem.at[3], rsem.at[3], 0, 16)
    dqkv_n[2] = jnp.dot(prob_b[...], ag_n[...], preferred_element_type=F32).astype(BF)

    scale = 1.0 / math.sqrt(HEAD)

    def backward(step, carry):
        i = lax.rem(x + step + 2, 4)
        at = pl.multiple_of(i * IB, IB)
        here = pl.ds(at, IB)
        g_part = ag_n[here, :]
        centre = jnp.sum(
            ag_t[:, here].astype(F32) * att_t[:, here].astype(F32), axis=0, keepdims=True
        )
        for b in range(8):
            rows = pl.ds(b * BLOCK, BLOCK)
            pg = lax.dot_general(qkv_r[2, rows, :], g_part, NT, preferred_element_type=F32)
            sgrad[rows, here] = (prob[i, rows, :] * ((pg - centre) * scale)).astype(BF)
        dq = jnp.dot(kt[...], sgrad[:, here], preferred_element_type=F32)
        dqkv_n[0, here, :] = dq.T.astype(BF)
        return carry

    def return_dq(step, carry):
        i = lax.rem(x + step + 2, 4)
        give_back(dqkv_n.at[0], dqkv_ret.at[0], ssem.at[4], rsem.at[4], 4 * i, 4)
        return carry

    def corner(p, edge):
        q = p // 2
        return (
            pl.ds(pl.multiple_of(16 * lax.rem(q, 4), 16), 16),
            pl.ds(pl.multiple_of(edge + 128 * (q // 4), 128), 128),
        )

    def to_planes(h):
        landed(ry.at[h], rsem.at[7 if h == 0 else 10])
        total = ry[h, 0].astype(F32) + ry[h, 1].astype(F32)
        total = total + ry[h, 2].astype(F32) + ry[h, 3].astype(F32)
        zsrc[h] = total.astype(BF)
        if planes == 1:
            zag[:, pl.ds(pl.multiple_of(512 * c + 256 * h, 256), 256)] = (
                total * (1.0 / 256.0)
            ).astype(BF)
            return

        def send_z(t, carry):
            zd = 2 * lax.rem(z // 2 + t + 4, planes // 2) + h
            rows, cols = corner(zd, 0)
            push(zsrc.at[h, rows, cols], zr.at[z], (2 * zd + c, seq), ssem.at[10], rsem.at[16])
            return carry

        lax.fori_loop(0, planes // 2, send_z, 0)

    lax.fori_loop(0, 1, backward, 0)
    learn(2)
    to_planes(0)
    give_back(dqkv_n.at[2], dqkv_ret.at[2], ssem.at[6], rsem.at[6], 0, 16)
    ring_forward(w_all, w_ssem, w_sem)
    lax.fori_loop(1, 2, backward, 0)
    to_planes(1)
    ring_relay(w_all, w_ssem, w_sem)
    lax.fori_loop(0, 2, return_dq, 0)
    lax.fori_loop(2, 4, backward, 0)
    lax.fori_loop(2, 4, return_dq, 0)
    dqkv_n[1] = jnp.dot(sgrad[...], qkv_r[0], preferred_element_type=F32).astype(BF)
    give_back(dqkv_n.at[1], dqkv_ret.at[1], ssem.at[5], rsem.at[5], 0, 16)

    if planes > 1:
        landed(zr, rsem.at[16])
        zsum = zr[0].astype(F32)
        for p in range(1, planes):
            zsum = zsum + zr[p].astype(F32)
        zres[...] = (zsum * (1.0 / 256.0)).astype(BF)
        parity = lax.rem(z, 2)
        rows, cols = corner(z, 512 * c + 256 * parity)

        def spread(t, carry):
            zd = lax.rem(z + t + planes // 2, planes)
            to = (2 * zd + c, seq)
            push(zres, zag.at[rows, cols], to, ssem.at[11], rsem.at[17 + parity])
            return carry

        lax.fori_loop(0, planes, spread, 0)

    ring_far(w_all, w_ssem, w_sem)
    landed(att_ret, rsem.at[3])
    ring_rest(w_all, w_sem)
    done = jnp.dot(
        att_ret[...].reshape(2 * ROWS, WIDTH),
        w_all[...].reshape(WIDTH, WIDTH),
        preferred_element_type=F32,
    ).astype(BF)
    out_ref[...] = jnp.swapaxes(done.reshape(2, ROWS, WIDTH), 0, 1)
    for i, ref in ((2, dv_ref), (0, dq_ref), (1, dk_ref)):
        landed(dqkv_ret.at[i], rsem.at[4 + i])
        ref[...] = jnp.swapaxes(dqkv_ret[i], 0, 1)

    for h in range(2):
        mine = zag.at[:, pl.ds(pl.multiple_of(512 * c + 256 * h, 256), 256)]
        if planes > 1:
            landed(mine, rsem.at[17 + h])
        send(mine, mine, sibling, ssem.at[12 + h], rsem.at[19 + h])
    for h in range(2):
        landed(zag.at[:, pl.ds(pl.multiple_of(512 - 512 * c + 256 * h, 256), 256)], rsem.at[19 + h])
    grad_ref[...] = zag[...].astype(F32)

    def left_here(sem, whole, short, is_short):
        @pl.when(is_short)
        def _():
            landed(short, sem)

        @pl.when(jnp.logical_not(is_short))
        def _():
            landed(whole, sem)

    @pl.when(own_side)
    def _():
        landed(aux, ssem.at[8])

    left_here(ssem.at[0], cot_s, cot_s.at[0], own_side)
    left_here(ssem.at[1], cot_s, cot_s.at[0], own_side)
    most = pl.ds(0, 15 * ROWS)
    left_here(ssem.at[2], qkv_r.at[0:2], qkv_r.at[0:2, most], own_side)
    left_here(ssem.at[9], qkv_r.at[2], qkv_r.at[2, most], own_side)
    left_here(ssem.at[3], att_n, att_n.at[most], own_side)
    for i in range(3):
        left_here(ssem.at[4 + i], dqkv_n.at[i], dqkv_n.at[i, most], own_side)
    left_here(ssem.at[7], ry, ry.at[:, pl.ds(0, 3)], own_side)
    if planes > 1:
        landed(zr.at[pl.ds(0, planes - 1)], ssem.at[10])
        landed(zr.at[pl.ds(0, planes - 1)], ssem.at[11])
    for h in range(2):
        landed(zag.at[:, pl.ds(256 * h, 256)], ssem.at[12 + h])
    ring_drain(cot_all, cot_ssem)
    ring_drain(w_all, w_ssem)


def finish(*refs):
    sem = refs[10]
    copies = [pltpu.make_async_copy(refs[i], refs[5 + i], sem.at[i]) for i in range(5)]
    for copy in copies:
        copy.start()
    for copy in copies:
        copy.wait()


def on_device(queries, key_rows, value_rows, cotangent, out_weight, node_counts, edge_bits):
    planes = lax.axis_size("dp") // 2
    hbm = pl.BlockSpec(memory_space=pltpu.HBM)
    vmem = pl.BlockSpec(memory_space=pltpu.VMEM)
    most_vmem = 48 * 1024 * 1024
    rows3 = jax.ShapeDtypeStruct((ROWS, 2, WIDTH), BF)
    grad = jax.ShapeDtypeStruct((ROWS, WIDTH), F32)
    dma = pltpu.SemaphoreType.DMA
    shapes = (rows3, rows3, rows3, rows3, grad)
    results = pl.pallas_call(
        functools.partial(kernel, planes),
        out_shape=tuple(pltpu.VMEM(one.shape, one.dtype) for one in shapes),
        in_specs=[hbm] * 7,
        out_specs=(vmem,) * 5,
        scratch_shapes=[
            pltpu.VMEM((4, ROWS, 2, WIDTH), BF),
            pltpu.VMEM((ROWS, WIDTH), BF),
            pltpu.SMEM((2,), jnp.int32),
            pltpu.SMEM((2, 8), jnp.int32),
            pltpu.VMEM((3, 2, ROWS, WIDTH), BF),
            pltpu.VMEM((2, ROWS, WIDTH), BF),
            pltpu.VMEM((3, NODES, HEAD), BF),
            pltpu.VMEM((16, NODES), F32),
            pltpu.VMEM((8, BLOCK, WIDTH), BF),
            pltpu.VMEM((8, BLOCK, WIDTH), BF),
            pltpu.VMEM((NODES, IB), F32),
            pltpu.VMEM((NODES // IB, NODES, IB), F32),
            pltpu.VMEM((NODES, NODES), BF),
            pltpu.VMEM((NODES, NODES), BF),
            pltpu.VMEM((HEAD, NODES), BF),
            pltpu.VMEM((NODES, HEAD), BF),
            pltpu.VMEM((NODES, HEAD), BF),
            pltpu.VMEM((HEAD, NODES), BF),
            pltpu.VMEM((HEAD, NODES), BF),
            pltpu.VMEM((HEAD, NODES), BF),
            pltpu.VMEM((3, NODES, HEAD), BF),
            pltpu.VMEM((2, ROWS, WIDTH), BF),
            pltpu.VMEM((3, 2, ROWS, WIDTH), BF),
            pltpu.VMEM((HEAD, WIDTH), BF),
            pltpu.VMEM((2, 4, ROWS, 256), BF),
            pltpu.VMEM((2, ROWS, 256), BF),
            pltpu.VMEM((16, 16, 128), BF),
            pltpu.VMEM((16, 128), BF),
            pltpu.VMEM((ROWS, WIDTH), BF),
            dma((7,)),
            dma((14,)),
            dma((21,)),
            dma((14,)),
            dma((14,)),
            dma((14,)),
            dma((14,)),
            pltpu.SemaphoreType.REGULAR((3,)),
        ],
        compiler_params=pltpu.CompilerParams(
            collective_id=0, has_side_effects=True, vmem_limit_bytes=most_vmem
        ),
        cost_estimate=pl.CostEstimate(
            flops=3_000_000_000, bytes_accessed=3_000_000, transcendentals=1_000_000
        ),
        name="sublayer",
    )(
        *[
            pltpu.with_memory_space_constraint(one, pltpu.HBM)
            for one in (
                queries,
                key_rows,
                value_rows,
                cotangent,
                out_weight,
                node_counts,
                edge_bits.reshape(2, 8),
            )
        ]
    )
    return pl.pallas_call(
        finish,
        out_shape=shapes,
        in_specs=[vmem] * 5,
        out_specs=(hbm,) * 5,
        scratch_shapes=[dma((5,))],
        compiler_params=pltpu.CompilerParams(vmem_limit_bytes=most_vmem),
        name="results",
    )(*results)


def solution(mesh):
    rows = P("seq", "dp", None)
    weight = P("seq", None)
    return jax.shard_map(
        on_device,
        mesh=mesh,
        in_specs=(rows, rows, rows, rows, weight, P("dp"), P("dp", None, None)),
        out_specs=(rows, rows, rows, rows, weight),
        check_vma=False,
    )
```

```python
import functools
import math

import jax
import jax.numpy as jnp
from jax import lax
from jax.experimental import pallas as pl
from jax.experimental.pallas import tpu as pltpu
from jax.sharding import PartitionSpec as P

HEAD = 128
BLOCK = 128
NODES = 1024
WIDTH = 1024
ROWS = 64
IB = 256
MESH = pl.DeviceIdType.MESH
BF = jnp.bfloat16
F32 = jnp.float32
NT = (((1,), (1,)), ((), ()))
MASKED = -1e30


def kernel(
    planes,
    q_ref,
    k_ref,
    v_ref,
    cot_ref,
    w_hbm,
    count_hbm,
    bits_hbm,
    out_ref,
    dq_ref,
    dk_ref,
    dv_ref,
    grad_ref,
    raw,
    w_ref,
    count_ref,
    bits_ref,
    qkv_s,
    cot_s,
    qkv_r,
    aux,
    cot_all,
    w_all,
    scores,
    prob,
    prob_b,
    sgrad,
    att_t,
    att_n,
    ag_n,
    ag_t,
    vt,
    kt,
    dqkv_n,
    att_ret,
    dqkv_ret,
    part,
    ry,
    zsrc,
    zr,
    zres,
    zag,
    in_sem,
    ssem,
    rsem,
    cot_sem,
    w_sem,
    cot_ssem,
    w_ssem,
    known,
):
    dp = lax.axis_index("dp")
    seq = lax.axis_index("seq")
    z, c = dp // 2, dp % 2
    x, y = seq // 4, seq % 4
    head = 2 * x + c
    own_side = c == y // 2

    def dev(xd, yd, cd):
        return (2 * z + cd, 4 * xd + yd)

    sibling = dev(x, y, 1 - c)

    incoming = [
        pltpu.make_async_copy(src, dst, in_sem.at[i])
        for i, (src, dst) in enumerate(
            (
                (cot_ref, raw.at[3]),
                (q_ref, raw.at[0]),
                (k_ref, raw.at[1]),
                (v_ref, raw.at[2]),
                (w_hbm, w_ref),
                (count_hbm, count_ref),
                (bits_hbm, bits_ref),
            )
        )
    ]
    for copy in incoming:
        copy.start()

    barrier = pltpu.get_barrier_semaphore()

    def greet(to):
        pl.semaphore_signal(barrier, inc=1, device_id=to, device_id_type=MESH)

    def greet_plane(t, carry):
        xd, j, cd = lax.rem(x + t // 4 + 2, 4), lax.rem(t // 2, 2), lax.rem(t, 2)
        to = dev(xd, 2 * c + j, cd)

        @pl.when(jnp.logical_not((to[0] == dp) & (to[1] == seq)))
        def _():
            greet(to)

        @pl.when(cd == 0)
        def _():
            greet(dev(xd, 2 * (1 - c) + j, y // 2))

        return carry

    def planes_at(distance):
        return (
            (2 * lax.rem(z + distance, planes) + c, seq),
            (2 * lax.rem(z + planes - distance, planes) + c, seq),
        )

    if planes > 1:
        for to in planes_at(1):
            greet(to)
    lax.fori_loop(0, 16, greet_plane, 0)

    @pl.when(jnp.logical_not(own_side))
    def _():
        greet(dev(lax.rem(x + 1, 4), y, c))
        greet(dev(lax.rem(x + 3, 4), y, c))

    incoming[0].wait()
    cot_s[...] = jnp.swapaxes(raw[3], 0, 1)
    for i in range(3):
        incoming[1 + i].wait()
        qkv_s[i] = jnp.swapaxes(raw[i], 0, 1)

    greeted = 2 if planes > 1 else 0

    @pl.when(own_side)
    def _():
        pl.semaphore_wait(barrier, 23 + greeted)

    @pl.when(jnp.logical_not(own_side))
    def _():
        pl.semaphore_wait(barrier, 26 + greeted)

    def tell(step):
        if planes > 1:
            for to in planes_at(2**step):
                pl.semaphore_signal(known.at[step], inc=1, device_id=to, device_id_type=MESH)

    def learn(step):
        if planes > 1:
            pl.semaphore_wait(known.at[step], 2)
            if step < 2:
                tell(step + 1)

    tell(0)

    def push(src, dst, to, s_sem, r_sem):
        same = (to[0] == dp) & (to[1] == seq)

        @pl.when(same)
        def _():
            pltpu.make_async_copy(src, dst, r_sem).start()

        @pl.when(jnp.logical_not(same))
        def _():
            pltpu.make_async_remote_copy(
                src, dst, s_sem, r_sem, device_id=to, device_id_type=MESH
            ).start()

    def send(src, dst, to, s_sem, r_sem):
        pltpu.make_async_remote_copy(
            src, dst, s_sem, r_sem, device_id=to, device_id_type=MESH
        ).start()

    def landed(ref, sem):
        pltpu.make_async_copy(ref, ref, sem).wait()

    half = pl.ds(ROWS * (y % 2), ROWS)
    for j in range(2):
        to = dev(x, 2 * c + j, y // 2)
        push(cot_s.at[j], cot_all.at[2 * x + y // 2, half], to, ssem.at[0], rsem.at[12 + y % 2])

    def send_qkv(first, count, sem):
        def one(t, carry):
            xd, j, cd = lax.rem(x + t // 4 + 2, 4), lax.rem(t // 2, 2), lax.rem(t, 2)
            cols = pl.ds(pl.multiple_of(HEAD * (2 * xd + cd), HEAD), HEAD)
            push(
                qkv_s.at[pl.ds(first, count), j, :, cols],
                qkv_r.at[pl.ds(first, count), pl.ds(pl.multiple_of(ROWS * seq, ROWS), ROWS), :],
                dev(xd, 2 * c + j, cd),
                ssem.at[sem],
                rsem.at[sem],
            )
            return carry

        lax.fori_loop(0, 16, one, 0)

    send_qkv(0, 2, 2)
    send_qkv(2, 1, 9)

    incoming[5].wait()
    incoming[6].wait()

    @pl.when(own_side)
    def _():
        count = count_ref[y % 2]
        key_block = lax.broadcasted_iota(jnp.int32, (8, BLOCK), 0)
        lane = lax.broadcasted_iota(jnp.int32, (8, BLOCK), 1)
        for i in range(8):
            bits = bits_ref[y % 2, i]
            seen = (jnp.right_shift(jnp.full((8, BLOCK), bits, jnp.int32), key_block) & 1) == 1
            limit = jnp.where(seen, count - BLOCK * key_block, 0)
            aux[0:8, i * BLOCK : (i + 1) * BLOCK] = limit.astype(F32)
            live = lane + i * BLOCK < count
            aux[8:16, i * BLOCK : (i + 1) * BLOCK] = jnp.where(live, 1.0, 0.0)
        send(aux, aux, sibling, ssem.at[8], rsem.at[8])

    incoming[4].wait()
    for j in range(2):
        to = dev(x, 2 * c + j, y // 2)
        push(w_ref, w_all.at[2 * x + y // 2, half], to, ssem.at[1], rsem.at[14 + y % 2])

    right = dev(lax.rem(x + 1, 4), y, c)
    left = dev(lax.rem(x + 3, 4), y, c)
    b_own = head
    b_left = 2 * lax.rem(x + 3, 4) + c
    b_right = 2 * lax.rem(x + 1, 4) + c
    b_far = 2 * lax.rem(x + 2, 4) + c
    low, high = pl.ds(0, ROWS), pl.ds(ROWS, ROWS)

    def ring_own(buf, s, r):
        for i, rows, to in (
            (0, low, right),
            (2, high, left),
            (1, high, right),
            (3, low, left),
            (6, low, sibling),
            (7, high, sibling),
        ):
            send(buf.at[b_own, rows], buf.at[b_own, rows], to, s.at[i], r.at[i])

    def ring_forward(buf, s, r):
        landed(buf.at[b_left, low], r.at[0])
        send(buf.at[b_left, low], buf.at[b_left, low], right, s.at[4], r.at[4])
        landed(buf.at[b_right, high], r.at[2])
        send(buf.at[b_right, high], buf.at[b_right, high], left, s.at[5], r.at[5])

    def ring_relay(buf, s, r):
        send(buf.at[b_left, low], buf.at[b_left, low], sibling, s.at[8], r.at[8])
        send(buf.at[b_right, high], buf.at[b_right, high], sibling, s.at[10], r.at[10])
        landed(buf.at[b_left, high], r.at[1])
        send(buf.at[b_left, high], buf.at[b_left, high], sibling, s.at[9], r.at[9])
        landed(buf.at[b_right, low], r.at[3])
        send(buf.at[b_right, low], buf.at[b_right, low], sibling, s.at[11], r.at[11])

    def ring_far(buf, s, r):
        landed(buf.at[b_far, low], r.at[4])
        send(buf.at[b_far, low], buf.at[b_far, low], sibling, s.at[12], r.at[12])
        landed(buf.at[b_far, high], r.at[5])
        send(buf.at[b_far, high], buf.at[b_far, high], sibling, s.at[13], r.at[13])

    def ring_rest(buf, r):
        other = 1 - 2 * c
        for i, b, rows in (
            (6, b_own, low),
            (7, b_own, high),
            (8, b_left, low),
            (9, b_left, high),
            (10, b_right, high),
            (11, b_right, low),
            (12, b_far, low),
            (13, b_far, high),
        ):
            landed(buf.at[b + other, rows], r.at[i])

    def ring_drain(buf, s):
        for i in range(14):
            landed(buf.at[0, low], s.at[i])

    landed(cot_all.at[b_own, low], rsem.at[12])
    landed(cot_all.at[b_own, high], rsem.at[13])
    ring_own(cot_all, cot_ssem, cot_sem)
    ring_forward(cot_all, cot_ssem, cot_sem)
    learn(0)

    @pl.when(jnp.logical_not(own_side))
    def _():
        landed(aux, rsem.at[8])

    landed(qkv_r.at[pl.ds(0, 2)], rsem.at[2])

    factor = math.log2(math.e) / math.sqrt(HEAD)
    key_pos = lax.broadcasted_iota(jnp.int32, (BLOCK, IB), 0).astype(F32)

    def forward(i, carry):
        at = pl.multiple_of(i * IB, IB)
        here = pl.ds(at, IB)
        q_part = qkv_r[0, here, :]
        top = jnp.full((8, IB), MASKED, F32)
        for b in range(8):
            rows = pl.ds(b * BLOCK, BLOCK)
            s = lax.dot_general(qkv_r[1, rows, :], q_part, NT, preferred_element_type=F32)
            s = jnp.where(key_pos < aux[b : b + 1, here], s * factor, MASKED)
            scores[rows, :] = s
            top = jnp.maximum(top, jnp.max(s.reshape(BLOCK // 8, 8, IB), axis=0))
        top = jnp.max(top, axis=0, keepdims=True)
        total = jnp.zeros((8, IB), F32)
        for b in range(8):
            rows = pl.ds(b * BLOCK, BLOCK)
            e = jnp.exp2(scores[rows, :] - top)
            scores[rows, :] = e
            total = total + jnp.sum(e.reshape(BLOCK // 8, 8, IB), axis=0)
        inverse = 1.0 / jnp.sum(total, axis=0, keepdims=True)
        for b in range(8):
            rows = pl.ds(b * BLOCK, BLOCK)
            p = scores[rows, :] * inverse
            prob[i, rows, :] = p
            prob_b[rows, here] = p.astype(BF)
        return carry

    lax.fori_loop(0, 4, forward, 0)
    learn(1)
    ring_relay(cot_all, cot_ssem, cot_sem)
    landed(w_all.at[b_own, low], rsem.at[14])
    landed(w_all.at[b_own, high], rsem.at[15])
    ring_own(w_all, w_ssem, w_sem)
    kt[...] = qkv_r[1].astype(F32).T.astype(BF)
    landed(qkv_r.at[pl.ds(2, 1)], rsem.at[9])
    vt[...] = qkv_r[2].astype(F32).T.astype(BF)

    def mix(i, carry):
        here = pl.ds(pl.multiple_of(i * IB, IB), IB)
        mixed = jnp.dot(vt[...], prob_b[:, here], preferred_element_type=F32)
        mixed = jnp.where(aux[8:9, here] > 0.5, mixed, 0.0)
        att_t[:, here] = mixed.astype(BF)
        att_n[here, :] = mixed.T.astype(BF)
        return carry

    lax.fori_loop(0, 4, mix, 0)

    my_cols = pl.ds(pl.multiple_of(HEAD * head, HEAD), HEAD)

    def give_back(src, dst, s_sem, r_sem, first, count):
        def one(t, carry):
            to = first + lax.rem(t + y + 2, 4) if count < 16 else lax.rem(seq + t + 8, 16)
            push(
                src.at[pl.ds(pl.multiple_of(ROWS * to, ROWS), ROWS), :],
                dst.at[y % 2, :, my_cols],
                (2 * z + y // 2, to),
                s_sem,
                r_sem,
            )
            return carry

        lax.fori_loop(0, count, one, 0)

    ring_far(cot_all, cot_ssem, cot_sem)
    ring_rest(cot_all, cot_sem)

    cot_rows = cot_all[...].reshape(NODES, WIDTH)
    for h in range(2):
        for cd in range(2):
            edge = 512 * cd + 256 * h
            part[:, edge : edge + 256] = jnp.dot(
                att_t[...], cot_rows[:, edge : edge + 256], preferred_element_type=F32
            ).astype(BF)
            for r in range(2):
                push(
                    part.at[pl.ds(ROWS * r, ROWS), pl.ds(edge, 256)],
                    ry.at[h, y],
                    dev(x, 2 * c + r, cd),
                    ssem.at[7],
                    rsem.at[7 if h == 0 else 10],
                )
    for b in range(8):
        rows = pl.ds(b * BLOCK, BLOCK)
        g = lax.dot_general(cot_all[b], w_all[b_own], NT, preferred_element_type=F32)
        gt = jnp.where(aux[8:9, b * BLOCK : (b + 1) * BLOCK] > 0.5, g.T, 0.0)
        ag_t[:, rows] = gt.astype(BF)
        ag_n[rows, :] = gt.T.astype(BF)

    give_back(att_n, att_ret, ssem.at[3], rsem.at[3], 0, 16)
    dqkv_n[2] = jnp.dot(prob_b[...], ag_n[...], preferred_element_type=F32).astype(BF)

    give_back(dqkv_n.at[2], dqkv_ret.at[2], ssem.at[6], rsem.at[6], 0, 16)

    scale = 1.0 / math.sqrt(HEAD)

    def backward(step, carry):
        i = lax.rem(x + step + 2, 4)
        at = pl.multiple_of(i * IB, IB)
        here = pl.ds(at, IB)
        g_part = ag_n[here, :]
        centre = jnp.sum(
            ag_t[:, here].astype(F32) * att_t[:, here].astype(F32), axis=0, keepdims=True
        )
        for b in range(8):
            rows = pl.ds(b * BLOCK, BLOCK)
            pg = lax.dot_general(qkv_r[2, rows, :], g_part, NT, preferred_element_type=F32)
            sgrad[rows, here] = (prob[i, rows, :] * ((pg - centre) * scale)).astype(BF)
        dq = jnp.dot(kt[...], sgrad[:, here], preferred_element_type=F32)
        dqkv_n[0, here, :] = dq.T.astype(BF)
        return carry

    def return_dq(step, carry):
        i = lax.rem(x + step + 2, 4)
        give_back(dqkv_n.at[0], dqkv_ret.at[0], ssem.at[4], rsem.at[4], 4 * i, 4)
        return carry

    def corner(p, edge):
        q = p // 2
        return (
            pl.ds(pl.multiple_of(16 * lax.rem(q, 4), 16), 16),
            pl.ds(pl.multiple_of(edge + 128 * (q // 4), 128), 128),
        )

    def to_planes(h):
        landed(ry.at[h], rsem.at[7 if h == 0 else 10])
        total = ry[h, 0].astype(F32) + ry[h, 1].astype(F32)
        total = total + ry[h, 2].astype(F32) + ry[h, 3].astype(F32)
        zsrc[h] = total.astype(BF)
        if planes == 1:
            zag[:, pl.ds(pl.multiple_of(512 * c + 256 * h, 256), 256)] = (
                total * (1.0 / 256.0)
            ).astype(BF)
            return

        def send_z(t, carry):
            zd = 2 * lax.rem(z // 2 + t + 4, planes // 2) + h
            rows, cols = corner(zd, 0)
            push(zsrc.at[h, rows, cols], zr.at[z], (2 * zd + c, seq), ssem.at[10], rsem.at[16])
            return carry

        lax.fori_loop(0, planes // 2, send_z, 0)

    lax.fori_loop(0, 1, backward, 0)
    learn(2)
    to_planes(0)
    ring_forward(w_all, w_ssem, w_sem)
    lax.fori_loop(1, 2, backward, 0)
    to_planes(1)
    ring_relay(w_all, w_ssem, w_sem)
    lax.fori_loop(0, 2, return_dq, 0)
    lax.fori_loop(2, 4, backward, 0)
    lax.fori_loop(2, 4, return_dq, 0)
    dqkv_n[1] = jnp.dot(sgrad[...], qkv_r[0], preferred_element_type=F32).astype(BF)
    give_back(dqkv_n.at[1], dqkv_ret.at[1], ssem.at[5], rsem.at[5], 0, 16)

    if planes > 1:
        landed(zr, rsem.at[16])
        zsum = zr[0].astype(F32)
        for p in range(1, planes):
            zsum = zsum + zr[p].astype(F32)
        zres[...] = (zsum * (1.0 / 256.0)).astype(BF)
        parity = lax.rem(z, 2)
        rows, cols = corner(z, 512 * c + 256 * parity)

        def spread(t, carry):
            zd = lax.rem(z + t + planes // 2, planes)
            to = (2 * zd + c, seq)
            push(zres, zag.at[rows, cols], to, ssem.at[11], rsem.at[17 + parity])
            return carry

        lax.fori_loop(0, planes, spread, 0)

    ring_far(w_all, w_ssem, w_sem)
    landed(att_ret, rsem.at[3])
    ring_rest(w_all, w_sem)
    done = jnp.dot(
        att_ret[...].reshape(2 * ROWS, WIDTH),
        w_all[...].reshape(WIDTH, WIDTH),
        preferred_element_type=F32,
    ).astype(BF)
    out_ref[...] = jnp.swapaxes(done.reshape(2, ROWS, WIDTH), 0, 1)
    for i, ref in ((2, dv_ref), (0, dq_ref), (1, dk_ref)):
        landed(dqkv_ret.at[i], rsem.at[4 + i])
        ref[...] = jnp.swapaxes(dqkv_ret[i], 0, 1)

    for h in range(2):
        mine = zag.at[:, pl.ds(pl.multiple_of(512 * c + 256 * h, 256), 256)]
        if planes > 1:
            landed(mine, rsem.at[17 + h])
        send(mine, mine, sibling, ssem.at[12 + h], rsem.at[19 + h])
    for h in range(2):
        landed(zag.at[:, pl.ds(pl.multiple_of(512 - 512 * c + 256 * h, 256), 256)], rsem.at[19 + h])
    grad_ref[...] = zag[...].astype(F32)

    def left_here(sem, whole, short, is_short):
        @pl.when(is_short)
        def _():
            landed(short, sem)

        @pl.when(jnp.logical_not(is_short))
        def _():
            landed(whole, sem)

    @pl.when(own_side)
    def _():
        landed(aux, ssem.at[8])

    left_here(ssem.at[0], cot_s, cot_s.at[0], own_side)
    left_here(ssem.at[1], cot_s, cot_s.at[0], own_side)
    most = pl.ds(0, 15 * ROWS)
    left_here(ssem.at[2], qkv_r.at[0:2], qkv_r.at[0:2, most], own_side)
    left_here(ssem.at[9], qkv_r.at[2], qkv_r.at[2, most], own_side)
    left_here(ssem.at[3], att_n, att_n.at[most], own_side)
    for i in range(3):
        left_here(ssem.at[4 + i], dqkv_n.at[i], dqkv_n.at[i, most], own_side)
    left_here(ssem.at[7], ry, ry.at[:, pl.ds(0, 3)], own_side)
    if planes > 1:
        landed(zr.at[pl.ds(0, planes - 1)], ssem.at[10])
        landed(zr.at[pl.ds(0, planes - 1)], ssem.at[11])
    for h in range(2):
        landed(zag.at[:, pl.ds(256 * h, 256)], ssem.at[12 + h])
    ring_drain(cot_all, cot_ssem)
    ring_drain(w_all, w_ssem)


def finish(*refs):
    sem = refs[10]
    copies = [pltpu.make_async_copy(refs[i], refs[5 + i], sem.at[i]) for i in range(5)]
    for copy in copies:
        copy.start()
    for copy in copies:
        copy.wait()


def on_device(queries, key_rows, value_rows, cotangent, out_weight, node_counts, edge_bits):
    planes = lax.axis_size("dp") // 2
    hbm = pl.BlockSpec(memory_space=pltpu.HBM)
    vmem = pl.BlockSpec(memory_space=pltpu.VMEM)
    most_vmem = 48 * 1024 * 1024
    rows3 = jax.ShapeDtypeStruct((ROWS, 2, WIDTH), BF)
    grad = jax.ShapeDtypeStruct((ROWS, WIDTH), F32)
    dma = pltpu.SemaphoreType.DMA
    shapes = (rows3, rows3, rows3, rows3, grad)
    results = pl.pallas_call(
        functools.partial(kernel, planes),
        out_shape=tuple(pltpu.VMEM(one.shape, one.dtype) for one in shapes),
        in_specs=[hbm] * 7,
        out_specs=(vmem,) * 5,
        scratch_shapes=[
            pltpu.VMEM((4, ROWS, 2, WIDTH), BF),
            pltpu.VMEM((ROWS, WIDTH), BF),
            pltpu.SMEM((2,), jnp.int32),
            pltpu.SMEM((2, 8), jnp.int32),
            pltpu.VMEM((3, 2, ROWS, WIDTH), BF),
            pltpu.VMEM((2, ROWS, WIDTH), BF),
            pltpu.VMEM((3, NODES, HEAD), BF),
            pltpu.VMEM((16, NODES), F32),
            pltpu.VMEM((8, BLOCK, WIDTH), BF),
            pltpu.VMEM((8, BLOCK, WIDTH), BF),
            pltpu.VMEM((NODES, IB), F32),
            pltpu.VMEM((NODES // IB, NODES, IB), F32),
            pltpu.VMEM((NODES, NODES), BF),
            pltpu.VMEM((NODES, NODES), BF),
            pltpu.VMEM((HEAD, NODES), BF),
            pltpu.VMEM((NODES, HEAD), BF),
            pltpu.VMEM((NODES, HEAD), BF),
            pltpu.VMEM((HEAD, NODES), BF),
            pltpu.VMEM((HEAD, NODES), BF),
            pltpu.VMEM((HEAD, NODES), BF),
            pltpu.VMEM((3, NODES, HEAD), BF),
            pltpu.VMEM((2, ROWS, WIDTH), BF),
            pltpu.VMEM((3, 2, ROWS, WIDTH), BF),
            pltpu.VMEM((HEAD, WIDTH), BF),
            pltpu.VMEM((2, 4, ROWS, 256), BF),
            pltpu.VMEM((2, ROWS, 256), BF),
            pltpu.VMEM((16, 16, 128), BF),
            pltpu.VMEM((16, 128), BF),
            pltpu.VMEM((ROWS, WIDTH), BF),
            dma((7,)),
            dma((14,)),
            dma((21,)),
            dma((14,)),
            dma((14,)),
            dma((14,)),
            dma((14,)),
            pltpu.SemaphoreType.REGULAR((3,)),
        ],
        compiler_params=pltpu.CompilerParams(
            collective_id=0, has_side_effects=True, vmem_limit_bytes=most_vmem
        ),
        cost_estimate=pl.CostEstimate(
            flops=3_000_000_000, bytes_accessed=3_000_000, transcendentals=1_000_000
        ),
        name="sublayer",
    )(
        *[
            pltpu.with_memory_space_constraint(one, pltpu.HBM)
            for one in (
                queries,
                key_rows,
                value_rows,
                cotangent,
                out_weight,
                node_counts,
                edge_bits.reshape(2, 8),
            )
        ]
    )
    return pl.pallas_call(
        finish,
        out_shape=shapes,
        in_specs=[vmem] * 5,
        out_specs=(hbm,) * 5,
        scratch_shapes=[dma((5,))],
        compiler_params=pltpu.CompilerParams(vmem_limit_bytes=most_vmem),
        name="results",
    )(*results)


def solution(mesh):
    rows = P("seq", "dp", None)
    weight = P("seq", None)
    return jax.shard_map(
        on_device,
        mesh=mesh,
        in_specs=(rows, rows, rows, rows, weight, P("dp"), P("dp", None, None)),
        out_specs=(rows, rows, rows, rows, weight),
        check_vma=False,
    )
```
